32 devices in a mesh: section: 2 (over core), dp: 16 (over z, y, x).
Axes of the slice: x: 2, y: 2, z: 4, core: 2. Of those that a mesh axis runs over, the one named last changes fastest.
Arguments:
- images: bfloat16 [4, 32, 8, 8, 512], P(None, 'dp'), may hold values from -6 to 6
- cotangent: bfloat16 [4, 32, 8, 8, 512], P(None, 'dp'), may hold values from -0.06591797 to 0.06591797
- counts: int32 [2], P('section'), may hold values from 1 to 4, as said below
- gains: float32 [8, 512], P('section'), may hold values from 0.1 to 1.9
- depthwise: float32 [8, 9, 512], P('section'), may hold values from -2 to 2
- pointwise: bfloat16 [8, 512, 512], P('section'), may hold values from -0.25 to 0.25
Outputs:
- grad_pointwise: float32 [8, 512, 512], P('section')
- grad_depthwise: float32 [8, 9, 512], P('section')
- grad_gains: float32 [8, 512], P('section')
The draws below stay inside these ranges and needn't reach their ends.
Inputs may be any that keep to these rules, and one draw needn't show every extreme that they name: counts[s] is how many cells segment s applies, from its first slot on; at least one segment applies 4 cells.
All inputs are finite; a program needn't handle non-finite values.
Results may differ from the reference program's by a relative error of at most 0.0085.
Values may be sent and summed in bfloat16 or wider, within the bound.
A program may use at most 64 MiB of HBM per device.

```python
import math
import jax
import jax.numpy as jnp
from jax import lax

C = 512
TAPS = 9
MAXC = 4
MICRO = 4
HEIGHT = 8
WIDTH = 8
BATCH = 32
SECTIONS = 2
SLOTS = 8


def draw_counts(key, part):
    key_counts, key_order = jax.random.split(key)
    drawn_counts = jax.random.randint(key_counts, (SECTIONS,), 1, MAXC + 1)
    shuffled = jax.random.permutation(key_order, SECTIONS)
    drawn_counts = drawn_counts.at[shuffled[0]].set(MAXC)
    return drawn_counts.astype(jnp.int32)


def shard_levels(own_key, shape, cuts, smallest, high):
    level, own = 1.0, jax.random.fold_in(own_key, 6)
    for position, blocks in cuts:
        draws = jnp.exp(jax.random.uniform(jax.random.fold_in(own, position), (blocks,), jnp.float32, smallest / len(cuts), high / len(cuts)))
        level = level * jnp.repeat(draws, shape[position] // blocks).reshape([-1 if axis == position else 1 for axis in range(len(shape))])
    return level


def centred(rng, dims, scale, limit, cuts=(), held_as=jnp.bfloat16):
    level = shard_levels(rng, dims, cuts, -0.22, 0.18) if cuts else 1.0
    values = jax.random.normal(rng, dims, jnp.float32) * scale * level
    return jnp.minimum(jnp.maximum(values, -limit), limit).astype(held_as)


def setup_inputs(seed: int = 0) -> dict:
    seeds = jax.random.split(jax.random.key(seed), 7)
    return {
        "images": centred(seeds[0], (MICRO, BATCH, HEIGHT, WIDTH, C), 1.0, 6.0, ((1, 16),)),
        "cotangent": centred(seeds[1], (MICRO, BATCH, HEIGHT, WIDTH, C), (1.0 / (MICRO * BATCH * HEIGHT * WIDTH) ** 0.5), 0.06591797, ((1, 16),)),
        "counts": draw_counts(jax.random.fold_in(seeds[6], 71), 0),
        "gains": jnp.clip(1.0 + 0.18 * jax.random.normal(seeds[3], (SLOTS, C), jnp.float32), 0.1, 1.9),
        "depthwise": centred(seeds[4], (SLOTS, TAPS, C), TAPS ** -0.5, 2.0, ((0, 2),), jnp.float32),
        "pointwise": centred(seeds[5], (SLOTS, C, C), C ** -0.5, 0.25, ((0, 2),)),
    }


EPSILON = 1e-06

def depth_apply(normed, depth_w):
    kernel = math.isqrt(depth_w.shape[0])
    offset = kernel // 2
    height, map_width = (normed.shape[1], normed.shape[2])
    padded = jnp.pad(normed, ((0, 0), (offset, offset), (offset, offset), (0, 0)))
    summed = jnp.zeros_like(normed)
    for row_tap in range(kernel):
        for col_tap in range(kernel):
            summed = summed + depth_w[row_tap * kernel + col_tap] * padded[:, row_tap:row_tap + height, col_tap:col_tap + map_width]
    return summed

def cell_parts(cell_in, gain_row, depth_w):
    widened = cell_in.astype(jnp.float32)
    inverse = lax.rsqrt(lax.optimization_barrier(jnp.mean(widened * widened, axis=-1, keepdims=True)) + EPSILON)
    normed = widened * inverse * gain_row
    linear = depth_apply(normed, depth_w)
    activated = (linear * jax.nn.sigmoid(linear)).astype(jnp.bfloat16)
    return (widened, inverse, normed, linear, activated)

def cell_forward(cell_in, gain_row, depth_w, point_w):
    widened, inverse, normed, linear, activated = cell_parts(cell_in, gain_row, depth_w)
    channels = point_w.shape[0]
    mixed_sum = jnp.dot(activated.reshape(-1, channels), point_w, preferred_element_type=jnp.float32)
    return (widened + mixed_sum.reshape(widened.shape)).astype(jnp.bfloat16)

def cell_backward(cell_in, grad_out, gain_row, depth_w, point_w):
    widened, inverse, normed, linear, activated = cell_parts(cell_in, gain_row, depth_w)
    channels = point_w.shape[0]
    flat_act = activated.reshape(-1, channels)
    flat_grad = grad_out.reshape(-1, channels)
    grad_point = lax.dot_general(flat_act, flat_grad, (((0,), (0,)), ((), ())), preferred_element_type=jnp.float32)
    grad_act = lax.dot_general(flat_grad, point_w, (((1,), (1,)), ((), ())), preferred_element_type=jnp.float32).reshape(widened.shape)
    sigma = jax.nn.sigmoid(linear)
    grad_linear = grad_act * (sigma * (1.0 + linear * (1.0 - sigma)))
    kernel = math.isqrt(depth_w.shape[0])
    offset = kernel // 2
    height, map_width = (normed.shape[1], normed.shape[2])
    padded = jnp.pad(normed, ((0, 0), (offset, offset), (offset, offset), (0, 0)))
    padded_grad = jnp.pad(grad_linear, ((0, 0), (offset, offset), (offset, offset), (0, 0)))
    tap_list = []
    grad_normed = jnp.zeros_like(grad_linear)
    for row_tap in range(kernel):
        for col_tap in range(kernel):
            tap_list.append(lax.optimization_barrier(jnp.sum(padded[:, row_tap:row_tap + height, col_tap:col_tap + map_width] * grad_linear, axis=(0, 1, 2))))
            row_start = 2 * offset - row_tap
            col_start = 2 * offset - col_tap
            grad_normed = grad_normed + depth_w[row_tap * kernel + col_tap] * padded_grad[:, row_start:row_start + height, col_start:col_start + map_width]
    grad_depth = jnp.stack(tap_list)
    grad_gain = lax.optimization_barrier(jnp.sum(grad_normed * widened * inverse, axis=(0, 1, 2)))
    scaled = grad_normed * gain_row
    grad_in = grad_out.astype(jnp.float32) + inverse * scaled - widened * inverse ** 3 * lax.optimization_barrier(jnp.mean(scaled * widened, axis=-1, keepdims=True))
    return (grad_in.astype(jnp.bfloat16), grad_point, grad_depth, grad_gain)

def reference(images, cotangent, counts, gains, depthwise, pointwise):
    item_shape = images.shape[2:]
    flat_in = images.reshape((-1,) + item_shape)
    flat_cot = cotangent.reshape((-1,) + item_shape)
    total_images = flat_in.shape[0]
    block = math.gcd(total_images, 32)
    blocks_in = flat_in.reshape((total_images // block, block) + item_shape)
    blocks_cot = flat_cot.reshape((total_images // block, block) + item_shape)

    def block_step(totals, pair):
        point_tot, depth_tot, gain_tot = totals
        running, grad_run = pair
        saved = []
        for slot_number in range(SLOTS):
            segment_number = slot_number // MAXC
            cell_number = slot_number % MAXC
            saved.append(running)
            moved = cell_forward(running, gains[slot_number], depthwise[slot_number], pointwise[slot_number])
            running = jnp.where(cell_number < counts[segment_number], moved, running)
        point_list = [None] * SLOTS
        depth_list = [None] * SLOTS
        gain_list = [None] * SLOTS
        for slot_number in reversed(range(SLOTS)):
            segment_number = slot_number // MAXC
            cell_number = slot_number % MAXC
            working = cell_number < counts[segment_number]
            grad_in, grad_point, grad_depth, grad_gain = cell_backward(saved[slot_number], grad_run, gains[slot_number], depthwise[slot_number], pointwise[slot_number])
            grad_run = jnp.where(working, grad_in, grad_run)
            point_list[slot_number] = jnp.where(working, grad_point, jnp.zeros_like(grad_point))
            depth_list[slot_number] = jnp.where(working, grad_depth, jnp.zeros_like(grad_depth))
            gain_list[slot_number] = jnp.where(working, grad_gain, jnp.zeros_like(grad_gain))
        return ((point_tot + jnp.stack(point_list), depth_tot + jnp.stack(depth_list), gain_tot + jnp.stack(gain_list)), None)
    start = (jnp.zeros((SLOTS, C, C), jnp.float32), jnp.zeros((SLOTS, TAPS, C), jnp.float32), jnp.zeros((SLOTS, C), jnp.float32))
    (point_sums, depth_sums, gain_sums), unused_out = lax.scan(block_step, start, (blocks_in, blocks_cot))
    return (point_sums, depth_sums, gain_sums)
```

```python
import functools

import jax
import jax.numpy as jnp
from jax import lax
from jax.experimental import pallas as pl
from jax.experimental.pallas import tpu as pltpu
from jax.sharding import PartitionSpec as P

MESH = pl.DeviceIdType.MESH
EPSILON = 1e-06
LANES = 128
TILE = 16
F32 = jnp.float32
BF16 = jnp.bfloat16
PACK_GAIN = 9
PACK_ACTIVE = 10


def kernel(
    plan,
    img,
    cot,
    pack_in,
    point_in,
    out,
    small_out,
    pack,
    point,
    xs,
    inv_all,
    normed_all,
    slope_all,
    act_all,
    gy,
    gl,
    taps,
    tap_acc,
    gain_acc,
    grads,
    reduced,
    from_core,
    small,
    small_recv,
    small_sum,
    send_sem,
    recv_sem,
    small_send,
    small_recv_sem,
    weight_send,
    weight_recv,
    load_sem,
    *landing,
):
    cells, slots, bits, halvings, height, image_rows, images = plan
    rows = images * image_rows
    channels = point.shape[-1]
    half = channels // 2
    blocks = channels // LANES
    core = lax.axis_index("section")
    me = lax.axis_index("dp")
    sibling = 1 - core

    digits = [lax.rem(me // (1 << b), 2) for b in range(bits)]
    weights = [1 << b for b in range(bits)]
    if bits >= 2:
        first, second = digits[0], digits[1]
        digits[0] = first + core * (second - first)
        digits[1] = second + core * (first - second)
        weights[0] = 1 + core
        weights[1] = 2 - core
    partners = [me + (1 - 2 * d) * w for d, w in zip(digits, weights)]
    base = core * half

    barrier = pltpu.get_barrier_semaphore()
    pl.semaphore_signal(barrier, inc=1, device_id=(sibling, me), device_id_type=MESH)
    for partner in partners:
        pl.semaphore_signal(barrier, inc=1, device_id=(core, partner), device_id_type=MESH)

    load_img = pltpu.make_async_copy(img.at[core], xs.at[0], load_sem.at[0])
    load_cot = pltpu.make_async_copy(cot.at[core], gy, load_sem.at[1])
    load_pack = pltpu.make_async_copy(pack_in, pack.at[pl.ds(core * cells, cells)], load_sem.at[2])
    load_img.start()
    load_pack.start()
    for j in range(cells):
        pltpu.make_async_copy(
            point_in.at[j], point.at[core * cells + j], weight_recv.at[core * cells + j]
        ).start()
    load_cot.start()
    pl.semaphore_wait(barrier, 1 + bits)

    def pack_copy():
        return pltpu.make_async_remote_copy(
            src_ref=pack_in,
            dst_ref=pack.at[pl.ds(core * cells, cells)],
            send_sem=load_sem.at[3],
            recv_sem=load_sem.at[4],
            device_id=(sibling, me),
            device_id_type=MESH,
        )

    def point_copy(j):
        return pltpu.make_async_remote_copy(
            src_ref=point_in.at[j],
            dst_ref=point.at[core * cells + j],
            send_sem=weight_send.at[j],
            recv_sem=weight_recv.at[core * cells + j],
            device_id=(sibling, me),
            device_id_type=MESH,
        )

    pack_copy().start()
    for j in range(cells):
        point_copy(j).start()
    load_img.wait()
    load_pack.wait()
    pack_copy().wait()

    column = lax.broadcasted_iota(jnp.int32, (8, channels), 0)

    def set_taps(k, low_tap_edge, high_tap_edge):
        for p in range(3):
            for q in range(3):
                t = p * 3 + q
                tile = jnp.broadcast_to(pack[k, t : t + 1, :], (8, channels))
                if q == 0:
                    tile = jnp.where(column == low_tap_edge, 0.0, tile)
                if q == 2:
                    tile = jnp.where(column == high_tap_edge, 0.0, tile)
                taps[t] = tile

    def lane(block):
        return slice(block * LANES, (block + 1) * LANES)

    def row_of(k, row, block, count):
        return jnp.broadcast_to(pack[k, row : row + 1, lane(block)], (count, LANES))

    def forward(k, carry):
        pltpu.make_async_copy(point.at[k], point.at[k], weight_recv.at[k]).wait()
        set_taps(k, 0, 7)

        def image(i, carry):
            at = pl.ds(pl.multiple_of(i * image_rows, image_rows), image_rows)
            xl = [xs[k, at, lane(b)].astype(F32) for b in range(blocks)]
            squares = sum(x * x for x in xl)
            mean = jnp.sum(squares, axis=1, keepdims=True) * (1.0 / channels)
            inv = jnp.broadcast_to(lax.rsqrt(mean + EPSILON), (image_rows, LANES))
            inv_all[k, at, :] = inv
            for b in range(blocks):
                normed = xl[b] * inv * row_of(k, PACK_GAIN, b, image_rows)
                normed_all[k, at, lane(b)] = normed
                mid = [normed[8 * h : 8 * h + 8] for h in range(height)]
                moved = [
                    [pltpu.roll(m, 1, axis=0) for m in mid],
                    mid,
                    [pltpu.roll(m, 7, axis=0) for m in mid],
                ]
                w = [taps[t, :, lane(b)] for t in range(9)]
                linear = []
                for h in range(height):
                    total = None
                    for p in range(3):
                        if 0 <= h + p - 1 < height:
                            for q in range(3):
                                term = w[p * 3 + q] * moved[q][h + p - 1]
                                total = term if total is None else total + term
                    linear.append(total)
                linear = jnp.concatenate(linear, axis=0)
                sigma = 0.5 * jnp.tanh(0.5 * linear) + 0.5
                act = linear * sigma
                act_all[k, at, lane(b)] = act.astype(BF16)
                slope_all[k, at, lane(b)] = sigma + act * (1.0 - sigma)
            return carry

        lax.fori_loop(0, images, image, 0)
        mixed = jnp.dot(act_all[k], point[k], preferred_element_type=F32)
        x = xs[k]
        y = (x.astype(F32) + mixed).astype(BF16)
        active = jnp.broadcast_to(pack[k, PACK_ACTIVE : PACK_ACTIVE + 1, :], (rows, channels))
        xs[k + 1] = jnp.where(active > 0.5, y.astype(F32), x.astype(F32)).astype(BF16)
        return carry

    lax.fori_loop(0, slots, forward, 0)
    load_cot.wait()
    for j in range(cells):
        point_copy(j).wait_send()

    def remote(src, dst, k, step, device):
        return pltpu.make_async_remote_copy(
            src_ref=src,
            dst_ref=dst,
            send_sem=send_sem.at[k, step],
            recv_sem=recv_sem.at[k, step],
            device_id=device,
            device_id_type=MESH,
        )

    def span(start, size):
        return pl.ds(pl.multiple_of(start, TILE), size)

    keep, away, sizes = [], [], []
    offset, size = base, half
    for b in range(bits):
        if b < halvings:
            size = size // 2
            away.append(offset + (1 - digits[b]) * size)
            offset = offset + digits[b] * size
        else:
            away.append(offset)
        keep.append(offset)
        sizes.append(size)

    def core_copy(k):
        return remote(
            grads.at[k, span(sibling * half, half)], from_core.at[k], k, 0, (sibling, me)
        )

    def scatter_copy(k, b):
        return remote(
            grads.at[k, span(away[b], sizes[b])], landing[b].at[k], k, 1 + b, (core, partners[b])
        )

    def gather_copy(k, b):
        part = span(keep[b], sizes[b])
        return remote(
            reduced.at[k, part], reduced.at[k, part], k, 1 + bits + b, (core, partners[b])
        )

    def home_copy(k):
        part = span(base, half)
        return remote(
            reduced.at[k, part],
            out.at[lax.rem(k, cells), part],
            k,
            1 + bits + halvings,
            (sibling, me),
        )

    def add_landed(k, part, landed):
        grads[k, part] = (grads[k, part].astype(F32) + landed.astype(F32)).astype(BF16)

    def finish(k):
        part = span(base, half)

        @pl.when(core != k // cells)
        def _():
            home_copy(k).start()

        @pl.when(core == k // cells)
        def _():
            out[lax.rem(k, cells), part] = reduced[k, part]

    def stage(k, age):
        if age <= 1 + bits:
            if age == 1:
                core_copy(k).wait()
                add_landed(k, span(base, half), from_core[k])
            else:
                b = age - 2
                scatter_copy(k, b).wait()
                add_landed(k, span(keep[b], sizes[b]), landing[b][k])
            if age <= bits:
                scatter_copy(k, age - 1).start()
            else:
                part = span(offset, size)
                reduced[k, part] = grads[k, part]
                if halvings:
                    gather_copy(k, halvings - 1).start()
                else:
                    finish(k)
        elif age <= 1 + bits + halvings:
            b = halvings - (age - 1 - bits)
            gather_copy(k, b).wait()
            if b > 0:
                gather_copy(k, b - 1).start()
            else:
                finish(k)
        else:

            @pl.when(core != k // cells)
            def _():
                home_copy(k).wait_send()

            @pl.when(core == k // cells)
            def _():
                home_copy(k).wait_recv()

    last_age = 2 + bits + halvings

    def small_copy(step):
        if step == 0:
            src, device = small.at[sibling], (sibling, me)
        else:
            src, device = small_sum.at[step - 1], (core, partners[step - 1])
        return pltpu.make_async_remote_copy(
            src_ref=src,
            dst_ref=small_recv.at[step],
            send_sem=small_send.at[step],
            recv_sem=small_recv_sem.at[step],
            device_id=device,
            device_id_type=MESH,
        )

    def small_stage(age):
        small_copy(age - 1).wait()
        own = small[core] if age == 1 else small_sum[age - 2]
        total = own + small_recv[age - 1]
        if age <= bits:
            small_sum[age - 1] = total
            small_copy(age).start()
        else:
            small_out[...] = total

    def backward(k):
        active = jnp.broadcast_to(
            pack[k, PACK_ACTIVE : PACK_ACTIVE + 1, :], (channels, channels)
        )
        gp = lax.dot_general(
            act_all[k], gy[...], (((0,), (0,)), ((), ())), preferred_element_type=F32
        )
        grads[k] = jnp.where(active > 0.5, gp, 0.0).astype(BF16)
        core_copy(k).start()
        ga = lax.dot_general(
            gy[...], point[k], (((1,), (1,)), ((), ())), preferred_element_type=F32
        )
        gl[...] = ga * slope_all[k]
        set_taps(k, 7, 0)
        tap_acc[...] = jnp.zeros_like(tap_acc)
        gain_acc[...] = jnp.zeros_like(gain_acc)

        def image(i, carry):
            at = pl.ds(pl.multiple_of(i * image_rows, image_rows), image_rows)
            inv = inv_all[k, at, :]
            gns = []
            for b in range(blocks):
                mid = [
                    gl[pl.ds(pl.multiple_of(i * image_rows + 8 * h, 8), 8), lane(b)]
                    for h in range(height)
                ]
                n = [
                    normed_all[
                        k, pl.ds(pl.multiple_of(i * image_rows + 8 * h, 8), 8), lane(b)
                    ]
                    for h in range(height)
                ]
                moved = [
                    [pltpu.roll(m, 7, axis=0) for m in mid],
                    mid,
                    [pltpu.roll(m, 1, axis=0) for m in mid],
                ]
                gn = [None] * height
                for p in range(3):
                    for q in range(3):
                        t = p * 3 + q
                        w = taps[t, :, lane(b)]
                        acc = tap_acc[t, :, lane(b)]
                        for h in range(height):
                            if 0 <= h - p + 1 < height:
                                piece = moved[q][h - p + 1]
                                term = w * piece
                                gn[h] = term if gn[h] is None else gn[h] + term
                                acc = acc + n[h] * piece
                        tap_acc[t, :, lane(b)] = acc
                gns.append(jnp.concatenate(gn, axis=0))
            dots = None
            us, xl = [], []
            for b in range(blocks):
                x = xs[k, at, lane(b)].astype(F32)
                term = gns[b] * x * inv
                gain_acc[:, lane(b)] += sum(term[8 * h : 8 * h + 8] for h in range(height))
                u = gns[b] * row_of(k, PACK_GAIN, b, image_rows)
                us.append(u)
                xl.append(x)
                dots = u * x if dots is None else dots + u * x
            mean = jnp.sum(dots, axis=1, keepdims=True) * (1.0 / channels)
            fall = jnp.broadcast_to(mean, (image_rows, LANES)) * (inv * inv * inv)
            for b in range(blocks):
                g = gy[at, lane(b)].astype(F32)
                gx = g + inv * us[b] - xl[b] * fall
                on = row_of(k, PACK_ACTIVE, b, image_rows) > 0.5
                gy[at, lane(b)] = jnp.where(on, gx, g).astype(BF16)
            return carry

        lax.fori_loop(0, images, image, 0)

        section, j = k // cells, lax.rem(k, cells)
        on = pack[k, PACK_ACTIVE : PACK_ACTIVE + 1, :] > 0.5
        sums = []
        for t in range(9):
            tile = tap_acc[t]
            if t % 3 == 0:
                tile = jnp.where(column == 7, 0.0, tile)
            if t % 3 == 2:
                tile = jnp.where(column == 0, 0.0, tile)
            sums.append(jnp.where(on, jnp.sum(tile, axis=0, keepdims=True), 0.0))
        gain = jnp.where(on, jnp.sum(gain_acc[...], axis=0, keepdims=True), 0.0)
        for t in range(8):
            small[section, j, t : t + 1, :] = sums[t]
        small[section, cells, pl.ds(j, 1), :] = sums[8]
        small[section, cells, pl.ds(cells + j, 1), :] = gain

    def tick(t, carry):
        for age in reversed(range(1, last_age + 1)):

            @pl.when((t >= age) & (t < age + slots))
            def _(age=age):
                stage(slots - 1 - (t - age), age)

        for age in range(1, bits + 2):

            @pl.when(t == slots - 1 + age)
            def _(age=age):
                small_stage(age)

        @pl.when(t < slots)
        def _():
            backward(slots - 1 - t)

        @pl.when(t == slots - 1)
        def _():
            small_copy(0).start()

        return carry

    lax.fori_loop(0, slots + last_age, tick, 0)


def local(images, cotangent, counts, gains, depthwise, pointwise):
    cells, channels = gains.shape
    sections = lax.axis_size("section")
    slots = sections * cells
    replicas = lax.axis_size("dp")
    bits = replicas.bit_length() - 1
    assert sections == 2 and replicas == 1 << bits and cells == 4
    micro, batch, height, width = images.shape[:4]
    assert width == 8 and depthwise.shape[1] == 9
    image_rows = height * width
    per_core = micro * batch // 2
    rows = per_core * image_rows
    half = channels // 2
    halvings = 0
    while halvings < bits and (half >> (halvings + 1)) % TILE == 0 and (half >> (halvings + 1)):
        halvings += 1

    img = images.reshape(2, rows, channels)
    cot = cotangent.reshape(2, rows, channels)
    active = (jnp.arange(cells) < counts[0]).astype(F32)[:, None, None]
    pack = jnp.concatenate(
        [
            depthwise,
            gains[:, None, :],
            jnp.broadcast_to(active, (cells, 1, channels)),
            jnp.zeros((cells, 5, channels), F32),
        ],
        axis=1,
    )
    landing = [
        pltpu.VMEM((slots, half >> min(b + 1, halvings), channels), BF16) for b in range(bits)
    ]
    steps = 2 + bits + halvings
    plan = (cells, slots, bits, halvings, height, image_rows, per_core)
    grid_rows = (cells + 1, 8, channels)
    moved, small = pl.pallas_call(
        functools.partial(kernel, plan),
        out_shape=(
            jax.ShapeDtypeStruct((cells, channels, channels), BF16),
            jax.ShapeDtypeStruct(grid_rows, F32),
        ),
        in_specs=[pl.BlockSpec(memory_space=pl.ANY)] * 4,
        out_specs=(
            pl.BlockSpec(memory_space=pltpu.VMEM),
            pl.BlockSpec(memory_space=pltpu.VMEM),
        ),
        scratch_shapes=[
            pltpu.VMEM((slots, 16, channels), F32),
            pltpu.VMEM((slots, channels, channels), BF16),
            pltpu.VMEM((slots + 1, rows, channels), BF16),
            pltpu.VMEM((slots, rows, LANES), F32),
            pltpu.VMEM((slots, rows, channels), F32),
            pltpu.VMEM((slots, rows, channels), F32),
            pltpu.VMEM((slots, rows, channels), BF16),
            pltpu.VMEM((rows, channels), BF16),
            pltpu.VMEM((rows, channels), F32),
            pltpu.VMEM((9, 8, channels), F32),
            pltpu.VMEM((9, 8, channels), F32),
            pltpu.VMEM((8, channels), F32),
            pltpu.VMEM((slots, channels, channels), BF16),
            pltpu.VMEM((slots, channels, channels), BF16),
            pltpu.VMEM((slots, half, channels), BF16),
            pltpu.VMEM((2,) + grid_rows, F32),
            pltpu.VMEM((bits + 1,) + grid_rows, F32),
            pltpu.VMEM((max(bits, 1),) + grid_rows, F32),
            pltpu.SemaphoreType.DMA((slots, steps)),
            pltpu.SemaphoreType.DMA((slots, steps)),
            pltpu.SemaphoreType.DMA((bits + 1,)),
            pltpu.SemaphoreType.DMA((bits + 1,)),
            pltpu.SemaphoreType.DMA((cells,)),
            pltpu.SemaphoreType.DMA((slots,)),
            pltpu.SemaphoreType.DMA((5,)),
        ]
        + landing,
        compiler_params=pltpu.CompilerParams(
            collective_id=0, has_side_effects=True, vmem_limit_bytes=56 * 1024 * 1024
        ),
    )(img, cot, pack, pointwise)
    depth = jnp.concatenate([small[:cells], small[cells, :cells][:, None, :]], axis=1)
    return (moved.astype(F32), depth, small[cells, cells:])


def solution(mesh):
    placed = (
        P(None, "dp", None, None, None),
        P(None, "dp", None, None, None),
        P("section"),
        P("section", None),
        P("section", None, None),
        P("section", None, None),
    )
    return jax.shard_map(
        local,
        mesh=mesh,
        in_specs=placed,
        out_specs=(P("section", None, None), P("section", None, None), P("section", None)),
        check_vma=False,
    )
```

```python
import functools

import jax
import jax.numpy as jnp
from jax import lax
from jax.experimental import pallas as pl
from jax.experimental.pallas import tpu as pltpu
from jax.sharding import PartitionSpec as P

MESH = pl.DeviceIdType.MESH
EPSILON = 1e-06
LANES = 128
TILE = 16
F32 = jnp.float32
BF16 = jnp.bfloat16


def kernel(
    plan,
    img,
    cot,
    counts,
    gains,
    depth_in,
    point_in,
    out,
    small_out,
    depth,
    meta,
    point,
    xs,
    inv_all,
    normed_all,
    slope_all,
    act_all,
    gy,
    gl,
    taps,
    tap_acc,
    gain_acc,
    grads,
    reduced,
    from_core,
    small,
    small_recv,
    small_sum,
    send_sem,
    recv_sem,
    small_send,
    small_recv_sem,
    weight_send,
    weight_recv,
    load_sem,
    *landing,
):
    cells, used, masked, bits, halvings, height, image_rows, images = plan
    slots = sum(used)
    rows = images * image_rows
    channels = point.shape[-1]
    half = channels // 2
    blocks = channels // LANES
    core = lax.axis_index("section")
    me = lax.axis_index("dp")
    sibling = 1 - core

    def owner(k):
        segment = (k + 8 - used[0]) // 8
        return segment, k - segment * used[0]

    digits = [lax.rem(me // (1 << b), 2) for b in range(bits)]
    weights = [1 << b for b in range(bits)]
    if bits >= 2:
        first, second = digits[0], digits[1]
        digits[0] = first + core * (second - first)
        digits[1] = second + core * (first - second)
        weights[0] = 1 + core
        weights[1] = 2 - core
    partners = [me + (1 - 2 * d) * w for d, w in zip(digits, weights)]
    base = core * half

    barrier = pltpu.get_barrier_semaphore()
    pl.semaphore_signal(barrier, inc=1, device_id=(sibling, me), device_id_type=MESH)
    for partner in partners:
        pl.semaphore_signal(barrier, inc=1, device_id=(core, partner), device_id_type=MESH)

    load_img = pltpu.make_async_copy(img.at[core], xs.at[0], load_sem.at[0])
    load_cot = pltpu.make_async_copy(cot.at[core], gy, load_sem.at[1])
    load_depth = pltpu.make_async_copy(
        depth_in, depth.at[pl.ds(core * cells, cells)], load_sem.at[2]
    )
    load_img.start()
    load_depth.start()

    def place(j):
        return core * used[0] + j

    def point_load(j):
        return pltpu.make_async_copy(
            point_in.at[j], point.at[place(j)], weight_recv.at[place(j)]
        )

    def each_cell(act):
        for j in range(cells):
            if j < min(used):
                act(j)
            elif j < max(used):

                @pl.when(core == (0 if used[0] > used[1] else 1))
                def _(j=j):
                    act(j)

    each_cell(lambda j: point_load(j).start())
    load_cot.start()
    for j in range(cells):
        meta[core, j : j + 1, :] = gains[j : j + 1, :]
        meta[core, cells + j : cells + j + 1, :] = jnp.where(
            jnp.full((1, channels), j, jnp.int32) < counts[0], 1.0, 0.0
        )
    pl.semaphore_wait(barrier, 1 + bits)

    def to_sibling(src, dst, send, recv):
        return pltpu.make_async_remote_copy(
            src_ref=src,
            dst_ref=dst,
            send_sem=send,
            recv_sem=recv,
            device_id=(sibling, me),
            device_id_type=MESH,
        )

    def depth_copy():
        return to_sibling(
            depth_in, depth.at[pl.ds(core * cells, cells)], load_sem.at[3], load_sem.at[4]
        )

    def meta_copy():
        return to_sibling(meta.at[core], meta.at[core], load_sem.at[5], load_sem.at[6])

    def point_copy(j):
        return to_sibling(
            point_in.at[j], point.at[place(j)], weight_send.at[j], weight_recv.at[place(j)]
        )

    depth_copy().start()
    meta_copy().start()
    each_cell(lambda j: point_copy(j).start())
    load_img.wait()
    load_depth.wait()
    depth_copy().wait()
    meta_copy().wait()

    column = lax.broadcasted_iota(jnp.int32, (8, channels), 0)

    def set_taps(k, low_tap_edge, high_tap_edge):
        segment, j = owner(k)
        for p in range(3):
            for q in range(3):
                t = p * 3 + q
                tile = jnp.broadcast_to(
                    depth[segment * cells + j, t : t + 1, :], (8, channels)
                )
                if q == 0:
                    tile = jnp.where(column == low_tap_edge, 0.0, tile)
                if q == 2:
                    tile = jnp.where(column == high_tap_edge, 0.0, tile)
                taps[t] = tile
        taps[9] = jnp.broadcast_to(meta[segment, pl.ds(j, 1), :], (8, channels))
        taps[10] = jnp.broadcast_to(meta[segment, pl.ds(cells + j, 1), :], (8, channels))

    def lane(block):
        return slice(block * LANES, (block + 1) * LANES)

    def stacked(tile, count):
        return jnp.concatenate([tile] * (count // 8), axis=0)

    def forward(k, carry):
        pltpu.make_async_copy(point.at[k], point.at[k], weight_recv.at[k]).wait()
        set_taps(k, 0, 7)

        def image(i, carry):
            at = pl.ds(pl.multiple_of(i * image_rows, image_rows), image_rows)
            xl = [xs[k, at, lane(b)].astype(F32) for b in range(blocks)]
            squares = sum(x * x for x in xl)
            mean = jnp.sum(squares, axis=1, keepdims=True) * (1.0 / channels)
            inv = jnp.broadcast_to(lax.rsqrt(mean + EPSILON), (image_rows, LANES))
            inv_all[k, at, :] = inv
            for b in range(blocks):
                normed = xl[b] * inv * stacked(taps[9, :, lane(b)], image_rows)
                normed_all[k, at, lane(b)] = normed
                mid = [normed[8 * h : 8 * h + 8] for h in range(height)]
                moved = [
                    [pltpu.roll(m, 1, axis=0) for m in mid],
                    mid,
                    [pltpu.roll(m, 7, axis=0) for m in mid],
                ]
                w = [taps[t, :, lane(b)] for t in range(9)]
                linear = []
                for h in range(height):
                    total = None
                    for p in range(3):
                        if 0 <= h + p - 1 < height:
                            for q in range(3):
                                term = w[p * 3 + q] * moved[q][h + p - 1]
                                total = term if total is None else total + term
                    linear.append(total)
                linear = jnp.concatenate(linear, axis=0)
                sigma = 0.5 * jnp.tanh(0.5 * linear) + 0.5
                act = linear * sigma
                act_all[k, at, lane(b)] = act.astype(BF16)
                slope_all[k, at, lane(b)] = sigma + act * (1.0 - sigma)
            return carry

        lax.fori_loop(0, images, image, 0)
        mixed = jnp.dot(act_all[k], point[k], preferred_element_type=F32)
        x = xs[k].astype(F32)
        y = x + mixed
        if masked:
            y = jnp.where(stacked(taps[10], rows) > 0.5, y, x)
        xs[k + 1] = y.astype(BF16)
        return carry

    lax.fori_loop(0, slots, forward, 0)
    load_cot.wait()
    each_cell(lambda j: point_copy(j).wait_send())

    def remote(src, dst, k, step, device):
        return pltpu.make_async_remote_copy(
            src_ref=src,
            dst_ref=dst,
            send_sem=send_sem.at[k, step],
            recv_sem=recv_sem.at[k, step],
            device_id=device,
            device_id_type=MESH,
        )

    def span(start, size):
        return pl.ds(pl.multiple_of(start, TILE), size)

    keep, away, sizes = [], [], []
    offset, size = base, half
    for b in range(bits):
        if b < halvings:
            size = size // 2
            away.append(offset + (1 - digits[b]) * size)
            offset = offset + digits[b] * size
        else:
            away.append(offset)
        keep.append(offset)
        sizes.append(size)

    def core_copy(k):
        return remote(
            grads.at[k, span(sibling * half, half)], from_core.at[k], k, 0, (sibling, me)
        )

    def scatter_copy(k, b):
        return remote(
            grads.at[k, span(away[b], sizes[b])], landing[b].at[k], k, 1 + b, (core, partners[b])
        )

    def gather_copy(k, b):
        part = span(keep[b], sizes[b])
        return remote(
            reduced.at[k, part], reduced.at[k, part], k, 1 + bits + b, (core, partners[b])
        )

    def home_copy(k):
        part = span(base, half)
        return remote(
            reduced.at[k, part],
            out.at[owner(k)[1], part],
            k,
            1 + bits + halvings,
            (sibling, me),
        )

    def add_landed(k, part, landed):
        grads[k, part] = (grads[k, part].astype(F32) + landed.astype(F32)).astype(BF16)

    def finish(k):
        part = span(base, half)
        segment, j = owner(k)

        @pl.when(core != segment)
        def _():
            home_copy(k).start()

        @pl.when(core == segment)
        def _():
            out[j, part] = reduced[k, part]

    def stage(k, age):
        if age <= bits:
            b = age - 1
            scatter_copy(k, b).wait()
            add_landed(k, span(keep[b], sizes[b]), landing[b][k])
            if age < bits:
                scatter_copy(k, age).start()
            else:
                part = span(offset, size)
                reduced[k, part] = grads[k, part]
                gather_copy(k, halvings - 1).start()
        else:
            b = halvings - (age - bits)
            gather_copy(k, b).wait()
            if b > 0:
                gather_copy(k, b - 1).start()
            else:
                finish(k)

    last_age = bits + halvings

    def pump(n, middle):
        ages = [a for a in range(1, last_age + 1) if a % 2 == (1 if middle else 0)]
        ages.sort(key=lambda a: sizes_of[a])
        for age in ages:
            turn = (age + 1) // 2 if middle else 1 + age // 2

            @pl.when((n >= turn) & (n < turn + slots))
            def _(age=age, turn=turn):
                stage(slots - 1 - (n - turn), age)

    sizes_of = {}
    for a in range(1, last_age + 1):
        sizes_of[a] = sizes[a - 1] if a <= bits else sizes[halvings - (a - bits)]

    def small_copy(step):
        if step == 0:
            src, device = small.at[sibling], (sibling, me)
        else:
            src, device = small_sum.at[step - 1], (core, partners[step - 1])
        return pltpu.make_async_remote_copy(
            src_ref=src,
            dst_ref=small_recv.at[step],
            send_sem=small_send.at[step],
            recv_sem=small_recv_sem.at[step],
            device_id=device,
            device_id_type=MESH,
        )

    def small_stage(age):
        small_copy(age - 1).wait()
        own = small[core] if age == 1 else small_sum[age - 2]
        total = own + small_recv[age - 1]
        if age <= bits:
            small_sum[age - 1] = total
            small_copy(age).start()
        else:
            small_out[...] = total

    small[...] = jnp.zeros_like(small)
    for j in range(cells):
        if j >= min(used):

            @pl.when(core == (0 if used[0] < used[1] else 1))
            def _(j=j):
                out[j] = jnp.zeros((channels, channels), BF16)

    def backward(n):
        k = slots - 1 - n
        gp = lax.dot_general(
            act_all[k], gy[...], (((0,), (0,)), ((), ())), preferred_element_type=F32
        )
        set_taps(k, 7, 0)
        if masked:
            gp = jnp.where(stacked(taps[10], channels) > 0.5, gp, 0.0)
        grads[k] = gp.astype(BF16)
        core_copy(k).start()
        ga = lax.dot_general(
            gy[...], point[k], (((1,), (1,)), ((), ())), preferred_element_type=F32
        )
        gl[...] = ga * slope_all[k]
        tap_acc[...] = jnp.zeros_like(tap_acc)
        gain_acc[...] = jnp.zeros_like(gain_acc)
        pump(n, True)

        def image(i, carry):
            at = pl.ds(pl.multiple_of(i * image_rows, image_rows), image_rows)
            inv = inv_all[k, at, :]
            gns = []
            for b in range(blocks):
                mid = [
                    gl[pl.ds(pl.multiple_of(i * image_rows + 8 * h, 8), 8), lane(b)]
                    for h in range(height)
                ]
                tiles = [
                    normed_all[
                        k, pl.ds(pl.multiple_of(i * image_rows + 8 * h, 8), 8), lane(b)
                    ]
                    for h in range(height)
                ]
                moved = [
                    [pltpu.roll(m, 7, axis=0) for m in mid],
                    mid,
                    [pltpu.roll(m, 1, axis=0) for m in mid],
                ]
                gn = [None] * height
                for p in range(3):
                    for q in range(3):
                        t = p * 3 + q
                        w = taps[t, :, lane(b)]
                        acc = tap_acc[t, :, lane(b)]
                        for h in range(height):
                            if 0 <= h - p + 1 < height:
                                piece = moved[q][h - p + 1]
                                term = w * piece
                                gn[h] = term if gn[h] is None else gn[h] + term
                                acc = acc + tiles[h] * piece
                        tap_acc[t, :, lane(b)] = acc
                gns.append(jnp.concatenate(gn, axis=0))
            dots = None
            us, xl = [], []
            for b in range(blocks):
                x = xs[k, at, lane(b)].astype(F32)
                term = gns[b] * x * inv
                gain_acc[:, lane(b)] += sum(term[8 * h : 8 * h + 8] for h in range(height))
                u = gns[b] * stacked(taps[9, :, lane(b)], image_rows)
                us.append(u)
                xl.append(x)
                dots = u * x if dots is None else dots + u * x
            mean = jnp.sum(dots, axis=1, keepdims=True) * (1.0 / channels)
            fall = jnp.broadcast_to(mean, (image_rows, LANES)) * (inv * inv * inv)
            for b in range(blocks):
                g = gy[at, lane(b)].astype(F32)
                gx = g + inv * us[b] - xl[b] * fall
                if masked:
                    gx = jnp.where(stacked(taps[10, :, lane(b)], image_rows) > 0.5, gx, g)
                gy[at, lane(b)] = gx.astype(BF16)
            return carry

        lax.fori_loop(0, images, image, 0)
        core_copy(k).wait()
        add_landed(k, span(base, half), from_core[k])
        scatter_copy(k, 0).start()

        segment, j = owner(k)
        on = taps[10, 0:1, :] > 0.5
        sums = []
        for t in range(9):
            tile = tap_acc[t]
            if t % 3 == 0:
                tile = jnp.where(column == 7, 0.0, tile)
            if t % 3 == 2:
                tile = jnp.where(column == 0, 0.0, tile)
            total = jnp.sum(tile, axis=0, keepdims=True)
            sums.append(jnp.where(on, total, 0.0) if masked else total)
        gain = jnp.sum(gain_acc[...], axis=0, keepdims=True)
        if masked:
            gain = jnp.where(on, gain, 0.0)
        for t in range(8):
            small[segment, j, t : t + 1, :] = sums[t]
        small[segment, cells, pl.ds(j, 1), :] = sums[8]
        small[segment, cells, pl.ds(cells + j, 1), :] = gain

    def turn(n, carry):
        pump(n, False)

        @pl.when(n < slots)
        def _():
            backward(n)

        @pl.when(n >= slots)
        def _():
            pump(n, True)

        @pl.when(n == slots - 1)
        def _():
            small_copy(0).start()

        for age in range(1, bits + 2):

            @pl.when(n == slots + (age - 1) // 2)
            def _(age=age):
                small_stage(age)

        return carry

    lax.fori_loop(0, slots + 1 + max(last_age // 2, (bits + 2) // 2), turn, 0)

    def wait_home(n, carry):
        k = slots - 1 - n
        segment, _ = owner(k)

        @pl.when(core != segment)
        def _():
            home_copy(k).wait_send()

        @pl.when(core == segment)
        def _():
            home_copy(k).wait_recv()

        return carry

    lax.fori_loop(0, slots, wait_home, 0)


def widen(moved, small, point_out, depth_out, gain_out):
    cells = gain_out.shape[0]
    point_out[...] = moved[...].astype(F32)

    @pl.when((pl.program_id(0) == 0) & (pl.program_id(1) == 0))
    def _():
        for j in range(cells):
            depth_out[j, 0:8, :] = small[j]
            depth_out[j, 8:9, :] = small[cells, j : j + 1, :]
        gain_out[...] = small[cells, cells : 2 * cells, :]


def local(images, cotangent, counts, gains, depthwise, pointwise):
    cells, channels = gains.shape
    sections = lax.axis_size("section")
    replicas = lax.axis_size("dp")
    bits = replicas.bit_length() - 1
    assert sections == 2 and replicas == 1 << bits and cells == 4
    micro, batch, height, width = images.shape[:4]
    assert width == 8 and depthwise.shape[1] == 9
    image_rows = height * width
    per_core = micro * batch // 2
    rows = per_core * image_rows
    half = channels // 2
    halvings = 0
    while halvings < bits and (half >> (halvings + 1)) % TILE == 0 and (half >> (halvings + 1)):
        halvings += 1

    img = images.reshape(2, rows, channels)
    cot = cotangent.reshape(2, rows, channels)
    used, masked = (cells, cells), True
    slots = sum(used)
    landing = [
        pltpu.VMEM((slots, half >> min(b + 1, halvings), channels), BF16) for b in range(bits)
    ]
    steps = 2 + bits + halvings
    plan = (cells, used, masked, bits, halvings, height, image_rows, per_core)
    grid_rows = (cells + 1, 8, channels)
    moved, small = pl.pallas_call(
        functools.partial(kernel, plan),
        out_shape=(
            jax.ShapeDtypeStruct((cells, channels, channels), BF16),
            jax.ShapeDtypeStruct(grid_rows, F32),
        ),
        in_specs=[pl.BlockSpec(memory_space=pl.ANY)] * 2
        + [pl.BlockSpec(memory_space=pltpu.SMEM), pl.BlockSpec(memory_space=pltpu.VMEM)]
        + [pl.BlockSpec(memory_space=pl.ANY)] * 2,
        out_specs=(
            pl.BlockSpec(memory_space=pltpu.VMEM),
            pl.BlockSpec(memory_space=pltpu.VMEM),
        ),
        scratch_shapes=[
            pltpu.VMEM((2 * cells, 9, channels), F32),
            pltpu.VMEM((2, 2 * cells, channels), F32),
            pltpu.VMEM((slots, channels, channels), BF16),
            pltpu.VMEM((slots + 1, rows, channels), BF16),
            pltpu.VMEM((slots, rows, LANES), F32),
            pltpu.VMEM((slots, rows, channels), F32),
            pltpu.VMEM((slots, rows, channels), F32),
            pltpu.VMEM((slots, rows, channels), BF16),
            pltpu.VMEM((rows, channels), BF16),
            pltpu.VMEM((rows, channels), F32),
            pltpu.VMEM((11, 8, channels), F32),
            pltpu.VMEM((9, 8, channels), F32),
            pltpu.VMEM((8, channels), F32),
            pltpu.VMEM((slots, channels, channels), BF16),
            pltpu.VMEM((slots, channels, channels), BF16),
            pltpu.VMEM((slots, half, channels), BF16),
            pltpu.VMEM((2,) + grid_rows, F32),
            pltpu.VMEM((bits + 1,) + grid_rows, F32),
            pltpu.VMEM((max(bits, 1),) + grid_rows, F32),
            pltpu.SemaphoreType.DMA((slots, steps)),
            pltpu.SemaphoreType.DMA((slots, steps)),
            pltpu.SemaphoreType.DMA((bits + 1,)),
            pltpu.SemaphoreType.DMA((bits + 1,)),
            pltpu.SemaphoreType.DMA((cells,)),
            pltpu.SemaphoreType.DMA((slots,)),
            pltpu.SemaphoreType.DMA((7,)),
        ]
        + landing,
        compiler_params=pltpu.CompilerParams(
            collective_id=0, has_side_effects=True, vmem_limit_bytes=48 * 1024 * 1024
        ),
    )(img, cot, counts, gains, depthwise, pointwise)
    whole = pl.BlockSpec(memory_space=pltpu.VMEM)
    block = pl.BlockSpec((1, half, channels), lambda j, i: (j, i, 0))
    return pl.pallas_call(
        widen,
        grid=(cells, 2),
        out_shape=(
            jax.ShapeDtypeStruct(pointwise.shape, F32),
            jax.ShapeDtypeStruct(depthwise.shape, F32),
            jax.ShapeDtypeStruct(gains.shape, F32),
        ),
        in_specs=[block, whole],
        out_specs=(block, whole, whole),
    )(moved, small)


def solution(mesh):
    placed = (
        P(None, "dp", None, None, None),
        P(None, "dp", None, None, None),
        P("section"),
        P("section", None),
        P("section", None, None),
        P("section", None, None),
    )
    return jax.shard_map(
        local,
        mesh=mesh,
        in_specs=placed,
        out_specs=(P("section", None, None), P("section", None, None), P("section", None)),
        check_vma=False,
    )
```

```python
import functools

import jax
import jax.numpy as jnp
from jax import lax
from jax.experimental import pallas as pl
from jax.experimental.pallas import tpu as pltpu
from jax.sharding import PartitionSpec as P

MESH = pl.DeviceIdType.MESH
EPSILON = 1e-06
LANES = 128
TILE = 16
F32 = jnp.float32
BF16 = jnp.bfloat16
PIECES = 4


def kernel(
    plan,
    img,
    cot,
    counts,
    gains,
    depth_in,
    point_in,
    out,
    depth_out,
    gain_out,
    depth,
    meta,
    point,
    xs,
    inv_all,
    normed_all,
    slope_all,
    act_all,
    gy,
    gl,
    taps,
    tap_acc,
    gain_acc,
    grads,
    reduced,
    from_core,
    small,
    small_recv,
    small_sum,
    send_sem,
    recv_sem,
    small_send,
    small_recv_sem,
    weight_send,
    weight_recv,
    load_sem,
    *landing,
):
    cells, used, masked, bits, height, image_rows, images = plan
    slots = sum(used)
    doublings = bits - 4
    rows = images * image_rows
    channels = point.shape[-1]
    half = channels // 2
    blocks = channels // LANES
    core = lax.axis_index("section")
    me = lax.axis_index("dp")
    sibling = 1 - core

    def owner(k):
        segment = (k + 8 - used[0]) // 8
        return segment, k - segment * used[0]

    digits = [lax.rem(me // (1 << b), 2) for b in range(bits)]
    weights = [1 << b for b in range(bits)]
    if bits >= 2:
        first, second = digits[0], digits[1]
        digits[0] = first + core * (second - first)
        digits[1] = second + core * (first - second)
        weights[0] = 1 + core
        weights[1] = 2 - core
    partners = [me + (1 - 2 * d) * w for d, w in zip(digits, weights)]
    base = core * half

    barrier = pltpu.get_barrier_semaphore()
    pl.semaphore_signal(barrier, inc=1, device_id=(sibling, me), device_id_type=MESH)
    ring = lax.rem(me // 4, 4)
    peers = [lax.rem(ring + r, 4) for r in range(4)]
    ring_partners = [me + (peer - ring) * 4 for peer in peers]
    for partner in partners[:2] + ring_partners[1:] + partners[4:]:
        pl.semaphore_signal(barrier, inc=1, device_id=(core, partner), device_id_type=MESH)

    load_img = pltpu.make_async_copy(img.at[core], xs.at[0], load_sem.at[0])
    load_cot = pltpu.make_async_copy(cot.at[core], gy, load_sem.at[1])
    load_depth = pltpu.make_async_copy(
        depth_in, depth.at[core], load_sem.at[2]
    )
    load_img.start()
    load_depth.start()

    def place(j):
        return core * used[0] + j

    def point_load(j):
        return pltpu.make_async_copy(
            point_in.at[j], point.at[place(j)], weight_recv.at[place(j)]
        )

    def each_cell(act):
        for j in range(cells):
            if j < min(used):
                act(j)
            elif j < max(used):

                @pl.when(core == (0 if used[0] > used[1] else 1))
                def _(j=j):
                    act(j)

    each_cell(lambda j: point_load(j).start())
    load_cot.start()
    for j in range(cells):
        meta[core, j : j + 1, :] = gains[j : j + 1, :]
        meta[core, cells + j : cells + j + 1, :] = jnp.where(
            jnp.full((1, channels), j, jnp.int32) < counts[0], 1.0, 0.0
        )
    pl.semaphore_wait(barrier, 2 + bits)

    def to_sibling(src, dst, send, recv):
        return pltpu.make_async_remote_copy(
            src_ref=src,
            dst_ref=dst,
            send_sem=send,
            recv_sem=recv,
            device_id=(sibling, me),
            device_id_type=MESH,
        )

    def depth_copy():
        return to_sibling(
            depth_in, depth.at[core], load_sem.at[3], load_sem.at[4]
        )

    def meta_copy():
        return to_sibling(meta.at[core], meta.at[core], load_sem.at[5], load_sem.at[6])

    def point_copy(j, part=slice(None)):
        return to_sibling(
            point_in.at[j, part],
            point.at[place(j), part],
            weight_send.at[j],
            weight_recv.at[place(j)],
        )

    def point_send(j):
        for piece in range(PIECES):
            point_copy(j, pl.ds(piece * (channels // PIECES), channels // PIECES)).start()

    depth_copy().start()
    meta_copy().start()
    each_cell(point_send)
    load_img.wait()
    load_depth.wait()
    depth_copy().wait()
    meta_copy().wait()

    column = lax.broadcasted_iota(jnp.int32, (8, channels), 0)

    def set_taps(k, low_tap_edge, high_tap_edge):
        segment, j = owner(k)
        for p in range(3):
            for q in range(3):
                t = p * 3 + q
                tile = jnp.broadcast_to(
                    depth[segment, t, pl.ds(j, 1), :], (8, channels)
                )
                if q == 0:
                    tile = jnp.where(column == low_tap_edge, 0.0, tile)
                if q == 2:
                    tile = jnp.where(column == high_tap_edge, 0.0, tile)
                taps[t] = tile
        taps[9] = jnp.broadcast_to(meta[segment, pl.ds(j, 1), :], (8, channels))
        taps[10] = jnp.broadcast_to(meta[segment, pl.ds(cells + j, 1), :], (8, channels))

    def lane(block):
        return slice(block * LANES, (block + 1) * LANES)

    def stacked(tile, count):
        return jnp.concatenate([tile] * (count // 8), axis=0)

    def forward(k, carry):
        pltpu.make_async_copy(point.at[k], point.at[k], weight_recv.at[k]).wait()
        set_taps(k, 0, 7)

        def image(i, carry):
            at = pl.ds(pl.multiple_of(i * image_rows, image_rows), image_rows)
            xl = [xs[k, at, lane(b)].astype(F32) for b in range(blocks)]
            squares = sum(x * x for x in xl)
            mean = jnp.sum(squares, axis=1, keepdims=True) * (1.0 / channels)
            inv = jnp.broadcast_to(lax.rsqrt(mean + EPSILON), (image_rows, LANES))
            inv_all[k, at, :] = inv
            for b in range(blocks):
                normed = xl[b] * inv * stacked(taps[9, :, lane(b)], image_rows)
                normed_all[k, at, lane(b)] = normed
                mid = [normed[8 * h : 8 * h + 8] for h in range(height)]
                moved = [
                    [pltpu.roll(m, 1, axis=0) for m in mid],
                    mid,
                    [pltpu.roll(m, 7, axis=0) for m in mid],
                ]
                w = [taps[t, :, lane(b)] for t in range(9)]
                linear = []
                for h in range(height):
                    total = None
                    for p in range(3):
                        if 0 <= h + p - 1 < height:
                            for q in range(3):
                                term = w[p * 3 + q] * moved[q][h + p - 1]
                                total = term if total is None else total + term
                    linear.append(total)
                linear = jnp.concatenate(linear, axis=0)
                sigma = 0.5 * jnp.tanh(0.5 * linear) + 0.5
                act = linear * sigma
                act_all[k, at, lane(b)] = act.astype(BF16)
                slope_all[k, at, lane(b)] = sigma + act * (1.0 - sigma)
            return carry

        lax.fori_loop(0, images, image, 0, unroll=2)
        mixed = jnp.dot(act_all[k], point[k], preferred_element_type=F32)
        x = xs[k].astype(F32)
        y = x + mixed
        if masked:
            y = jnp.where(stacked(taps[10], rows) > 0.5, y, x)
        xs[k + 1] = y.astype(BF16)
        return carry

    lax.fori_loop(0, slots, forward, 0)
    load_cot.wait()
    each_cell(lambda j: point_copy(j).wait_send())

    def remote(src, dst, k, step, device):
        return pltpu.make_async_remote_copy(
            src_ref=src,
            dst_ref=dst,
            send_sem=send_sem.at[k, step],
            recv_sem=recv_sem.at[k, step],
            device_id=device,
            device_id_type=MESH,
        )

    def span(start, size):
        return pl.ds(pl.multiple_of(start, TILE), size)

    keep, away, sizes = [], [], []
    offset, size = base, half
    for b in range(2):
        size = size // 2
        away.append(offset + (1 - digits[b]) * size)
        offset = offset + digits[b] * size
        keep.append(offset)
        sizes.append(size)
    size = size // 4
    own = offset + ring * size

    def pieces(make, start, size, count):
        for piece in range(count):
            make(start + piece * (size // count), size // count).start()

    def core_copy(k, start, size):
        return remote(
            grads.at[k, span(sibling * half + start, size)],
            from_core.at[k, span(start, size)],
            k,
            0,
            (sibling, me),
        )

    def pair_copy(k, b, start, size):
        return remote(
            grads.at[k, span(away[b] + start, size)],
            landing[b].at[k, span(start, size)],
            k,
            1 + b,
            (core, partners[b]),
        )

    def send_pair(k, b):
        pieces(lambda start, size: pair_copy(k, b, start, size), 0, sizes[b], 2)

    def ring_copy(k, r):
        return remote(
            grads.at[k, span(offset + peers[r] * size, size)],
            landing[2].at[k, r - 1],
            k,
            2 + r,
            (core, ring_partners[r]),
        )

    def double_copy(k, d):
        return remote(
            grads.at[k, span(own, size)], landing[3 + d].at[k], k, 9 + d, (core, partners[4 + d])
        )

    def spread_copy(k, r):
        part = span(own, size)
        return remote(
            reduced.at[k, part],
            reduced.at[k, part],
            k,
            5 + r,
            (core, ring_partners[r]),
        )

    def gather_copy(k, b, start, size):
        part = span(keep[b] + start, size)
        return remote(
            reduced.at[k, part], reduced.at[k, part], k, 9 + doublings + b, (core, partners[b])
        )

    def send_gather(k, b):
        pieces(lambda start, size: gather_copy(k, b, start, size), 0, sizes[b], 2)

    def home_copy(k, start, size):
        part = span(base + start, size)
        return remote(
            reduced.at[k, part],
            out.at[owner(k)[1], part],
            k,
            11 + doublings,
            (sibling, me),
        )

    def add_landed(k, part, *landed):
        total = grads[k, part].astype(F32)
        for block in landed:
            total = total + block.astype(F32)
        grads[k, part] = total.astype(BF16)

    def spread(k):
        part = span(own, size)
        reduced[k, part] = grads[k, part]
        for r in range(1, 4):
            spread_copy(k, r).start()

    def finish(k):
        part = span(base, half)
        segment, j = owner(k)

        @pl.when(core != segment)
        def _():
            pieces(lambda start, size: home_copy(k, start, size), 0, half, PIECES)

        @pl.when(core == segment)
        def _():
            out[j, part] = reduced[k, part]

    last_age = 7 + doublings

    def stage(k, age):
        if age == 1:
            core_copy(k, 0, half).wait()
            add_landed(k, span(base, half), from_core[k])
            send_pair(k, 0)
        elif age <= 3:
            b = age - 2
            pair_copy(k, b, 0, sizes[b]).wait()
            add_landed(k, span(keep[b], sizes[b]), landing[b][k])
            if b == 0:
                send_pair(k, 1)
            else:
                for r in range(1, 4):
                    ring_copy(k, r).start()
        elif age <= 4 + doublings:
            d = age - 4
            if d == 0:
                for r in range(1, 4):
                    ring_copy(k, r).wait()
                add_landed(k, span(own, size), *[landing[2][k, r] for r in range(3)])
            else:
                double_copy(k, d - 1).wait()
                add_landed(k, span(own, size), landing[2 + d][k])
            if d < doublings:
                double_copy(k, d).start()
            else:
                spread(k)
        elif age == 5 + doublings:
            for r in range(1, 4):
                spread_copy(k, r).wait()
            send_gather(k, 1)
        elif age == 6 + doublings:
            gather_copy(k, 1, 0, sizes[1]).wait()
            send_gather(k, 0)
        else:
            gather_copy(k, 0, 0, sizes[0]).wait()
            finish(k)

    def pump(n):
        order = list(range(4, 6 + doublings)) + [3, 6 + doublings, 2, 7 + doublings, 1]
        for age in order:

            @pl.when((n >= age) & (n < age + slots))
            def _(age=age):
                stage(slots - 1 - (n - age), age)

    def small_copy(step):
        if step == 0:
            src, device = small.at[sibling], (sibling, me)
        else:
            src, device = small_sum.at[step - 1], (core, partners[step - 1])
        return pltpu.make_async_remote_copy(
            src_ref=src,
            dst_ref=small_recv.at[step],
            send_sem=small_send.at[step],
            recv_sem=small_recv_sem.at[step],
            device_id=device,
            device_id_type=MESH,
        )

    def small_stage(age):
        small_copy(age - 1).wait()
        own = small[core] if age == 1 else small_sum[age - 2]
        total = own + small_recv[age - 1]
        if age <= bits:
            small_sum[age - 1] = total
            small_copy(age).start()
        else:
            for j in range(cells):
                for t in range(8):
                    depth_out[t, j : j + 1, :] = total[j, t : t + 1, :]
            depth_out[8] = total[cells, :cells]
            gain_out[...] = total[cells, cells:]

    small[...] = jnp.zeros_like(small)
    for j in range(cells):
        if j >= min(used):

            @pl.when(core == (0 if used[0] < used[1] else 1))
            def _(j=j):
                out[j] = jnp.zeros((channels, channels), BF16)

    def backward(n):
        k = slots - 1 - n
        gp = lax.dot_general(
            act_all[k], gy[...], (((0,), (0,)), ((), ())), preferred_element_type=F32
        )
        set_taps(k, 7, 0)
        if masked:
            gp = jnp.where(stacked(taps[10], channels) > 0.5, gp, 0.0)
        grads[k] = gp.astype(BF16)
        pieces(lambda start, size: core_copy(k, start, size), 0, half, PIECES)
        ga = lax.dot_general(
            gy[...], point[k], (((1,), (1,)), ((), ())), preferred_element_type=F32
        )
        gl[...] = ga * slope_all[k]
        tap_acc[...] = jnp.zeros_like(tap_acc)
        gain_acc[...] = jnp.zeros_like(gain_acc)

        def image(i, carry):
            at = pl.ds(pl.multiple_of(i * image_rows, image_rows), image_rows)
            inv = inv_all[k, at, :]
            gns = []
            for b in range(blocks):
                mid = [
                    gl[pl.ds(pl.multiple_of(i * image_rows + 8 * h, 8), 8), lane(b)]
                    for h in range(height)
                ]
                tiles = [
                    normed_all[
                        k, pl.ds(pl.multiple_of(i * image_rows + 8 * h, 8), 8), lane(b)
                    ]
                    for h in range(height)
                ]
                moved = [
                    [pltpu.roll(m, 7, axis=0) for m in mid],
                    mid,
                    [pltpu.roll(m, 1, axis=0) for m in mid],
                ]
                gn = [None] * height
                for p in range(3):
                    for q in range(3):
                        t = p * 3 + q
                        w = taps[t, :, lane(b)]
                        acc = tap_acc[t, :, lane(b)]
                        for h in range(height):
                            if 0 <= h - p + 1 < height:
                                piece = moved[q][h - p + 1]
                                term = w * piece
                                gn[h] = term if gn[h] is None else gn[h] + term
                                acc = acc + tiles[h] * piece
                        tap_acc[t, :, lane(b)] = acc
                gns.append(jnp.concatenate(gn, axis=0))
            dots = None
            us, xl = [], []
            for b in range(blocks):
                x = xs[k, at, lane(b)].astype(F32)
                term = gns[b] * x * inv
                gain_acc[:, lane(b)] += sum(term[8 * h : 8 * h + 8] for h in range(height))
                u = gns[b] * stacked(taps[9, :, lane(b)], image_rows)
                us.append(u)
                xl.append(x)
                dots = u * x if dots is None else dots + u * x
            mean = jnp.sum(dots, axis=1, keepdims=True) * (1.0 / channels)
            fall = jnp.broadcast_to(mean, (image_rows, LANES)) * (inv * inv * inv)
            for b in range(blocks):
                g = gy[at, lane(b)].astype(F32)
                gx = g + inv * us[b] - xl[b] * fall
                if masked:
                    gx = jnp.where(stacked(taps[10, :, lane(b)], image_rows) > 0.5, gx, g)
                gy[at, lane(b)] = gx.astype(BF16)
            return carry

        lax.fori_loop(0, images, image, 0, unroll=2)

        segment, j = owner(k)
        on = taps[10, 0:1, :] > 0.5
        sums = []
        for t in range(9):
            tile = tap_acc[t]
            if t % 3 == 0:
                tile = jnp.where(column == 7, 0.0, tile)
            if t % 3 == 2:
                tile = jnp.where(column == 0, 0.0, tile)
            total = jnp.sum(tile, axis=0, keepdims=True)
            sums.append(jnp.where(on, total, 0.0) if masked else total)
        gain = jnp.sum(gain_acc[...], axis=0, keepdims=True)
        if masked:
            gain = jnp.where(on, gain, 0.0)
        for t in range(8):
            small[segment, j, t : t + 1, :] = sums[t]
        small[segment, cells, pl.ds(j, 1), :] = sums[8]
        small[segment, cells, pl.ds(cells + j, 1), :] = gain

    def turn(n, carry):
        pump(n)

        @pl.when(n < slots)
        def _():
            backward(n)

        @pl.when(n == slots - 1)
        def _():
            small_copy(0).start()

        for age in range(1, bits + 2):

            @pl.when(n == slots - 1 + age)
            def _(age=age):
                small_stage(age)

        return carry

    lax.fori_loop(0, slots + max(last_age, bits + 1), turn, 0)

    def wait_home(n, carry):
        k = slots - 1 - n
        segment, _ = owner(k)

        @pl.when(core != segment)
        def _():
            home_copy(k, 0, half).wait_send()

        @pl.when(core == segment)
        def _():
            home_copy(k, 0, half).wait_recv()

        return carry

    lax.fori_loop(0, slots, wait_home, 0)


def local(images, cotangent, counts, gains, depthwise, pointwise):
    cells, channels = gains.shape
    sections = lax.axis_size("section")
    replicas = lax.axis_size("dp")
    bits = replicas.bit_length() - 1
    assert sections == 2 and replicas == 1 << bits and cells == 4
    micro, batch, height, width = images.shape[:4]
    assert width == 8 and depthwise.shape[1] == 9
    image_rows = height * width
    per_core = micro * batch // 2
    rows = per_core * image_rows
    half = channels // 2
    assert bits >= 4 and half % (16 * TILE) == 0

    img = images.reshape(2, rows, channels)
    cot = cotangent.reshape(2, rows, channels)
    used, masked = (cells, cells), True
    slots = sum(used)
    piece = half // 16
    landing = [
        pltpu.VMEM((slots, half // 2, channels), BF16),
        pltpu.VMEM((slots, half // 4, channels), BF16),
        pltpu.VMEM((slots, 3, piece, channels), BF16),
    ] + [pltpu.VMEM((slots, piece, channels), BF16)] * (bits - 4)
    steps = 8 + bits
    plan = (cells, used, masked, bits, height, image_rows, per_core)
    grid_rows = (cells + 1, 8, channels)
    point, depth, gain = pl.pallas_call(
        functools.partial(kernel, plan),
        out_shape=(
            jax.ShapeDtypeStruct((cells, channels, channels), BF16),
            jax.ShapeDtypeStruct((9, cells, channels), F32),
            jax.ShapeDtypeStruct((cells, channels), F32),
        ),
        in_specs=[pl.BlockSpec(memory_space=pl.ANY)] * 2
        + [pl.BlockSpec(memory_space=pltpu.SMEM), pl.BlockSpec(memory_space=pltpu.VMEM)]
        + [pl.BlockSpec(memory_space=pl.ANY)] * 2,
        out_specs=(pl.BlockSpec(memory_space=pltpu.VMEM),) * 3,
        scratch_shapes=[
            pltpu.VMEM((2, 9, cells, channels), F32),
            pltpu.VMEM((2, 2 * cells, channels), F32),
            pltpu.VMEM((slots, channels, channels), BF16),
            pltpu.VMEM((slots + 1, rows, channels), BF16),
            pltpu.VMEM((slots, rows, LANES), F32),
            pltpu.VMEM((slots, rows, channels), F32),
            pltpu.VMEM((slots, rows, channels), F32),
            pltpu.VMEM((slots, rows, channels), BF16),
            pltpu.VMEM((rows, channels), BF16),
            pltpu.VMEM((rows, channels), F32),
            pltpu.VMEM((11, 8, channels), F32),
            pltpu.VMEM((9, 8, channels), F32),
            pltpu.VMEM((8, channels), F32),
            pltpu.VMEM((slots, channels, channels), BF16),
            pltpu.VMEM((slots, channels, channels), BF16),
            pltpu.VMEM((slots, half, channels), BF16),
            pltpu.VMEM((2,) + grid_rows, F32),
            pltpu.VMEM((bits + 1,) + grid_rows, F32),
            pltpu.VMEM((max(bits, 1),) + grid_rows, F32),
            pltpu.SemaphoreType.DMA((slots, steps)),
            pltpu.SemaphoreType.DMA((slots, steps)),
            pltpu.SemaphoreType.DMA((bits + 1,)),
            pltpu.SemaphoreType.DMA((bits + 1,)),
            pltpu.SemaphoreType.DMA((cells,)),
            pltpu.SemaphoreType.DMA((slots,)),
            pltpu.SemaphoreType.DMA((7,)),
        ]
        + landing,
        compiler_params=pltpu.CompilerParams(
            collective_id=0, has_side_effects=True, vmem_limit_bytes=60 * 1024 * 1024
        ),
    )(img, cot, counts, gains, depthwise.transpose(1, 0, 2), pointwise)
    return (point.astype(F32), depth.transpose(1, 0, 2), gain)


def solution(mesh):
    placed = (
        P(None, "dp", None, None, None),
        P(None, "dp", None, None, None),
        P("section"),
        P("section", None),
        P("section", None, None),
        P("section", None, None),
    )
    return jax.shard_map(
        local,
        mesh=mesh,
        in_specs=placed,
        out_specs=(P("section", None, None), P("section", None, None), P("section", None)),
        check_vma=False,
    )
```

```python
import functools

import jax
import jax.numpy as jnp
from jax import lax
from jax.experimental import pallas as pl
from jax.experimental.pallas import tpu as pltpu
from jax.sharding import PartitionSpec as P

MESH = pl.DeviceIdType.MESH
EPSILON = 1e-06
LANES = 128
TILE = 16
F32 = jnp.float32
BF16 = jnp.bfloat16
PIECES = 4


def kernel(
    plan,
    img,
    cot,
    counts,
    gains,
    depth_in,
    point_in,
    out,
    depth_out,
    gain_out,
    depth,
    meta,
    point,
    xs,
    inv_all,
    normed_all,
    slope_all,
    act_all,
    gy,
    gl,
    taps,
    tap_acc,
    gain_acc,
    grads,
    reduced,
    from_core,
    small,
    small_recv,
    small_sum,
    send_sem,
    recv_sem,
    small_send,
    small_recv_sem,
    weight_send,
    weight_recv,
    load_sem,
    *landing,
):
    cells, used, masked, bits, height, image_rows, images = plan
    slots = sum(used)
    doublings = bits - 4
    rows = images * image_rows
    channels = point.shape[-1]
    half = channels // 2
    blocks = channels // LANES
    core = lax.axis_index("section")
    me = lax.axis_index("dp")
    sibling = 1 - core

    def owner(k):
        segment = (k + 8 - used[0]) // 8
        return segment, k - segment * used[0]

    digits = [lax.rem(me // (1 << b), 2) for b in range(bits)]
    weights = [1 << b for b in range(bits)]
    if bits >= 2:
        first, second = digits[0], digits[1]
        digits[0] = first + core * (second - first)
        digits[1] = second + core * (first - second)
        weights[0] = 1 + core
        weights[1] = 2 - core
    partners = [me + (1 - 2 * d) * w for d, w in zip(digits, weights)]
    base = core * half

    barrier = pltpu.get_barrier_semaphore()
    for home in (me, partners[1]):
        pl.semaphore_signal(barrier, inc=1, device_id=(sibling, home), device_id_type=MESH)
    ring = lax.rem(me // 4, 4)
    peers = [lax.rem(ring + r, 4) for r in range(4)]
    ring_partners = [me + (peer - ring) * 4 for peer in peers]
    for partner in partners[:2] + ring_partners[1:] + partners[4:]:
        pl.semaphore_signal(barrier, inc=1, device_id=(core, partner), device_id_type=MESH)

    load_img = pltpu.make_async_copy(img.at[core], xs.at[0], load_sem.at[0])
    load_cot = pltpu.make_async_copy(cot.at[core], gy, load_sem.at[1])
    load_depth = pltpu.make_async_copy(
        depth_in, depth.at[core], load_sem.at[2]
    )
    load_img.start()
    load_depth.start()

    def place(j):
        return core * used[0] + j

    def point_load(j):
        return pltpu.make_async_copy(
            point_in.at[j], point.at[place(j)], weight_recv.at[place(j)]
        )

    def each_cell(act):
        for j in range(cells):
            if j < min(used):
                act(j)
            elif j < max(used):

                @pl.when(core == (0 if used[0] > used[1] else 1))
                def _(j=j):
                    act(j)

    each_cell(lambda j: point_load(j).start())
    load_cot.start()
    for j in range(cells):
        meta[core, j : j + 1, :] = gains[j : j + 1, :]
        meta[core, cells + j : cells + j + 1, :] = jnp.where(
            jnp.full((1, channels), j, jnp.int32) < counts[0], 1.0, 0.0
        )
    pl.semaphore_wait(barrier, 3 + bits)

    def to_sibling(src, dst, send, recv):
        return pltpu.make_async_remote_copy(
            src_ref=src,
            dst_ref=dst,
            send_sem=send,
            recv_sem=recv,
            device_id=(sibling, me),
            device_id_type=MESH,
        )

    def depth_copy():
        return to_sibling(
            depth_in, depth.at[core], load_sem.at[3], load_sem.at[4]
        )

    def meta_copy():
        return to_sibling(meta.at[core], meta.at[core], load_sem.at[5], load_sem.at[6])

    def point_copy(j, part=slice(None)):
        return to_sibling(
            point_in.at[j, part],
            point.at[place(j), part],
            weight_send.at[j],
            weight_recv.at[place(j)],
        )

    def point_send(j):
        for piece in range(PIECES):
            point_copy(j, pl.ds(piece * (channels // PIECES), channels // PIECES)).start()

    depth_copy().start()
    meta_copy().start()
    each_cell(point_send)
    load_img.wait()
    load_depth.wait()
    depth_copy().wait()
    meta_copy().wait()

    column = lax.broadcasted_iota(jnp.int32, (8, channels), 0)

    def set_taps(k, low_tap_edge, high_tap_edge):
        segment, j = owner(k)
        for p in range(3):
            for q in range(3):
                t = p * 3 + q
                tile = jnp.broadcast_to(
                    depth[segment, t, pl.ds(j, 1), :], (8, channels)
                )
                if q == 0:
                    tile = jnp.where(column == low_tap_edge, 0.0, tile)
                if q == 2:
                    tile = jnp.where(column == high_tap_edge, 0.0, tile)
                taps[t] = tile
        taps[9] = jnp.broadcast_to(meta[segment, pl.ds(j, 1), :], (8, channels))
        taps[10] = jnp.broadcast_to(meta[segment, pl.ds(cells + j, 1), :], (8, channels))

    def lane(block):
        return slice(block * LANES, (block + 1) * LANES)

    def stacked(tile, count):
        return jnp.concatenate([tile] * (count // 8), axis=0)

    def forward(k, carry):
        pltpu.make_async_copy(point.at[k], point.at[k], weight_recv.at[k]).wait()
        set_taps(k, 0, 7)

        def image(i, carry):
            at = pl.ds(pl.multiple_of(i * image_rows, image_rows), image_rows)
            xl = [xs[k, at, lane(b)].astype(F32) for b in range(blocks)]
            squares = sum(x * x for x in xl)
            mean = jnp.sum(squares, axis=1, keepdims=True) * (1.0 / channels)
            inv = jnp.broadcast_to(lax.rsqrt(mean + EPSILON), (image_rows, LANES))
            inv_all[k, at, :] = inv
            for b in range(blocks):
                normed = xl[b] * inv * stacked(taps[9, :, lane(b)], image_rows)
                normed_all[k, at, lane(b)] = normed
                mid = [normed[8 * h : 8 * h + 8] for h in range(height)]
                moved = [
                    [pltpu.roll(m, 1, axis=0) for m in mid],
                    mid,
                    [pltpu.roll(m, 7, axis=0) for m in mid],
                ]
                w = [taps[t, :, lane(b)] for t in range(9)]
                linear = []
                for h in range(height):
                    total = None
                    for p in range(3):
                        if 0 <= h + p - 1 < height:
                            for q in range(3):
                                term = w[p * 3 + q] * moved[q][h + p - 1]
                                total = term if total is None else total + term
                    linear.append(total)
                linear = jnp.concatenate(linear, axis=0)
                sigma = 0.5 * jnp.tanh(0.5 * linear) + 0.5
                act = linear * sigma
                act_all[k, at, lane(b)] = act.astype(BF16)
                slope_all[k, at, lane(b)] = sigma + act * (1.0 - sigma)
            return carry

        lax.fori_loop(0, images, image, 0, unroll=2)
        mixed = jnp.dot(act_all[k], point[k], preferred_element_type=F32)
        x = xs[k].astype(F32)
        y = x + mixed
        if masked:
            y = jnp.where(stacked(taps[10], rows) > 0.5, y, x)
        xs[k + 1] = y.astype(BF16)
        return carry

    lax.fori_loop(0, slots, forward, 0)
    load_cot.wait()
    each_cell(lambda j: point_copy(j).wait_send())

    def remote(src, dst, k, step, device):
        return pltpu.make_async_remote_copy(
            src_ref=src,
            dst_ref=dst,
            send_sem=send_sem.at[k, step],
            recv_sem=recv_sem.at[k, step],
            device_id=device,
            device_id_type=MESH,
        )

    def span(start, size):
        return pl.ds(pl.multiple_of(start, TILE), size)

    keep, away, sizes = [], [], []
    offset, size = base, half
    for b in range(2):
        size = size // 2
        away.append(offset + (1 - digits[b]) * size)
        offset = offset + digits[b] * size
        keep.append(offset)
        sizes.append(size)
    size = size // 4
    own = offset + ring * size

    def pieces(make, start, size, count):
        for piece in range(count):
            make(start + piece * (size // count), size // count).start()

    def core_copy(k, start, size):
        return remote(
            grads.at[k, span(sibling * half + start, size)],
            from_core.at[k, span(start, size)],
            k,
            0,
            (sibling, me),
        )

    def pair_copy(k, b, start, size):
        return remote(
            grads.at[k, span(away[b] + start, size)],
            landing[b].at[k, span(start, size)],
            k,
            1 + b,
            (core, partners[b]),
        )

    def send_pair(k, b):
        pieces(lambda start, size: pair_copy(k, b, start, size), 0, sizes[b], 2)

    def ring_copy(k, r):
        return remote(
            grads.at[k, span(offset + peers[r] * size, size)],
            landing[2].at[k, r - 1],
            k,
            2 + r,
            (core, ring_partners[r]),
        )

    def double_copy(k, d):
        return remote(
            grads.at[k, span(own, size)], landing[3 + d].at[k], k, 9 + d, (core, partners[4 + d])
        )

    def spread_copy(k, r):
        part = span(own, size)
        return remote(
            reduced.at[k, part],
            reduced.at[k, part],
            k,
            5 + r,
            (core, ring_partners[r]),
        )

    def gather_copy(k, b, start, size):
        part = span(keep[b] + start, size)
        return remote(
            reduced.at[k, part], reduced.at[k, part], k, 9 + doublings + b, (core, partners[b])
        )

    def send_gather(k, b):
        pieces(lambda start, size: gather_copy(k, b, start, size), 0, sizes[b], 2)

    homes = (me, partners[0])

    def home_copy(k, to, start, size):
        part = span(keep[0] + start, size)
        return remote(
            reduced.at[k, part],
            out.at[owner(k)[1], part],
            k,
            11 + doublings + to,
            (sibling, homes[to]),
        )

    def add_landed(k, part, *landed):
        total = grads[k, part].astype(F32)
        for block in landed:
            total = total + block.astype(F32)
        grads[k, part] = total.astype(BF16)

    def spread(k):
        part = span(own, size)
        reduced[k, part] = grads[k, part]
        for r in range(1, 4):
            spread_copy(k, r).start()

    def owned(k):
        return core == owner(k)[0]

    def send_home(k):
        @pl.when(owned(k))
        def _():
            send_gather(k, 0)

        @pl.when(core != owner(k)[0])
        def _():
            for to in (1, 0):
                pieces(
                    lambda start, size: home_copy(k, to, start, size), 0, sizes[0], PIECES // 2
                )

    def finish(k):
        @pl.when(owned(k))
        def _():
            part = span(base, half)
            gather_copy(k, 0, 0, sizes[0]).wait()
            out[owner(k)[1], part] = reduced[k, part]

    last_age = 7 + doublings

    def stage(k, age):
        if age == 1:
            core_copy(k, 0, half).wait()
            add_landed(k, span(base, half), from_core[k])
            send_pair(k, 0)
        elif age <= 3:
            b = age - 2
            pair_copy(k, b, 0, sizes[b]).wait()
            add_landed(k, span(keep[b], sizes[b]), landing[b][k])
            if b == 0:
                send_pair(k, 1)
            else:
                for r in range(1, 4):
                    ring_copy(k, r).start()
        elif age <= 4 + doublings:
            d = age - 4
            if d == 0:
                for r in range(1, 4):
                    ring_copy(k, r).wait()
                add_landed(k, span(own, size), *[landing[2][k, r] for r in range(3)])
            else:
                double_copy(k, d - 1).wait()
                add_landed(k, span(own, size), landing[2 + d][k])
            if d < doublings:
                double_copy(k, d).start()
            else:
                spread(k)
        elif age == 5 + doublings:
            for r in range(1, 4):
                spread_copy(k, r).wait()
            send_gather(k, 1)
        elif age == 6 + doublings:
            gather_copy(k, 1, 0, sizes[1]).wait()
            send_home(k)
        else:
            finish(k)

    def pump(n):
        order = list(range(4, 6 + doublings)) + [3, 6 + doublings, 2, 7 + doublings, 1]
        for age in order:

            @pl.when((n >= age) & (n < age + slots))
            def _(age=age):
                stage(slots - 1 - (n - age), age)

    def small_copy(step):
        if step == 0:
            src, device = small.at[sibling], (sibling, me)
        else:
            src, device = small_sum.at[step - 1], (core, partners[step - 1])
        return pltpu.make_async_remote_copy(
            src_ref=src,
            dst_ref=small_recv.at[step],
            send_sem=small_send.at[step],
            recv_sem=small_recv_sem.at[step],
            device_id=device,
            device_id_type=MESH,
        )

    def small_stage(age):
        small_copy(age - 1).wait()
        own = small[core] if age == 1 else small_sum[age - 2]
        total = own + small_recv[age - 1]
        if age <= bits:
            small_sum[age - 1] = total
            small_copy(age).start()
        else:
            for j in range(cells):
                for t in range(8):
                    depth_out[t, j : j + 1, :] = total[j, t : t + 1, :]
            depth_out[8] = total[cells, :cells]
            gain_out[...] = total[cells, cells:]

    small[...] = jnp.zeros_like(small)
    for j in range(cells):
        if j >= min(used):

            @pl.when(core == (0 if used[0] < used[1] else 1))
            def _(j=j):
                out[j] = jnp.zeros((channels, channels), BF16)

    def backward(n):
        k = slots - 1 - n
        gp = lax.dot_general(
            act_all[k], gy[...], (((0,), (0,)), ((), ())), preferred_element_type=F32
        )
        set_taps(k, 7, 0)
        if masked:
            gp = jnp.where(stacked(taps[10], channels) > 0.5, gp, 0.0)
        grads[k] = gp.astype(BF16)
        pieces(lambda start, size: core_copy(k, start, size), 0, half, PIECES)
        ga = lax.dot_general(
            gy[...], point[k], (((1,), (1,)), ((), ())), preferred_element_type=F32
        )
        gl[...] = ga * slope_all[k]
        tap_acc[...] = jnp.zeros_like(tap_acc)
        gain_acc[...] = jnp.zeros_like(gain_acc)

        def image(i, carry):
            at = pl.ds(pl.multiple_of(i * image_rows, image_rows), image_rows)
            inv = inv_all[k, at, :]
            gns = []
            for b in range(blocks):
                mid = [
                    gl[pl.ds(pl.multiple_of(i * image_rows + 8 * h, 8), 8), lane(b)]
                    for h in range(height)
                ]
                tiles = [
                    normed_all[
                        k, pl.ds(pl.multiple_of(i * image_rows + 8 * h, 8), 8), lane(b)
                    ]
                    for h in range(height)
                ]
                moved = [
                    [pltpu.roll(m, 7, axis=0) for m in mid],
                    mid,
                    [pltpu.roll(m, 1, axis=0) for m in mid],
                ]
                gn = [None] * height
                for p in range(3):
                    for q in range(3):
                        t = p * 3 + q
                        w = taps[t, :, lane(b)]
                        acc = tap_acc[t, :, lane(b)]
                        for h in range(height):
                            if 0 <= h - p + 1 < height:
                                piece = moved[q][h - p + 1]
                                term = w * piece
                                gn[h] = term if gn[h] is None else gn[h] + term
                                acc = acc + tiles[h] * piece
                        tap_acc[t, :, lane(b)] = acc
                gns.append(jnp.concatenate(gn, axis=0))
            dots = None
            us, xl = [], []
            for b in range(blocks):
                x = xs[k, at, lane(b)].astype(F32)
                term = gns[b] * x * inv
                gain_acc[:, lane(b)] += sum(term[8 * h : 8 * h + 8] for h in range(height))
                u = gns[b] * stacked(taps[9, :, lane(b)], image_rows)
                us.append(u)
                xl.append(x)
                dots = u * x if dots is None else dots + u * x
            mean = jnp.sum(dots, axis=1, keepdims=True) * (1.0 / channels)
            fall = jnp.broadcast_to(mean, (image_rows, LANES)) * (inv * inv * inv)
            for b in range(blocks):
                g = gy[at, lane(b)].astype(F32)
                gx = g + inv * us[b] - xl[b] * fall
                if masked:
                    gx = jnp.where(stacked(taps[10, :, lane(b)], image_rows) > 0.5, gx, g)
                gy[at, lane(b)] = gx.astype(BF16)
            return carry

        lax.fori_loop(0, images, image, 0, unroll=2)

        segment, j = owner(k)
        on = taps[10, 0:1, :] > 0.5
        sums = []
        for t in range(9):
            tile = tap_acc[t]
            if t % 3 == 0:
                tile = jnp.where(column == 7, 0.0, tile)
            if t % 3 == 2:
                tile = jnp.where(column == 0, 0.0, tile)
            total = jnp.sum(tile, axis=0, keepdims=True)
            sums.append(jnp.where(on, total, 0.0) if masked else total)
        gain = jnp.sum(gain_acc[...], axis=0, keepdims=True)
        if masked:
            gain = jnp.where(on, gain, 0.0)
        for t in range(8):
            small[segment, j, t : t + 1, :] = sums[t]
        small[segment, cells, pl.ds(j, 1), :] = sums[8]
        small[segment, cells, pl.ds(cells + j, 1), :] = gain

    def turn(n, carry):
        pump(n)

        @pl.when(n < slots)
        def _():
            backward(n)

        @pl.when(n == slots - 1)
        def _():
            small_copy(0).start()

        for age in range(1, bits + 2):

            @pl.when(n == slots - 1 + age)
            def _(age=age):
                small_stage(age)

        return carry

    lax.fori_loop(0, slots + max(last_age, bits + 1), turn, 0)

    def wait_home(n, carry):
        k = slots - 1 - n
        for to in (0, 1):

            @pl.when(core != owner(k)[0])
            def _(to=to):
                home_copy(k, to, 0, sizes[0]).wait_send()

            @pl.when(owned(k))
            def _(to=to):
                home_copy(k, to, 0, sizes[0]).wait_recv()

        return carry

    lax.fori_loop(0, slots, wait_home, 0)


def local(images, cotangent, counts, gains, depthwise, pointwise):
    cells, channels = gains.shape
    sections = lax.axis_size("section")
    replicas = lax.axis_size("dp")
    bits = replicas.bit_length() - 1
    assert sections == 2 and replicas == 1 << bits and cells == 4
    micro, batch, height, width = images.shape[:4]
    assert width == 8 and depthwise.shape[1] == 9
    image_rows = height * width
    per_core = micro * batch // 2
    rows = per_core * image_rows
    half = channels // 2
    assert bits >= 4 and half % (16 * TILE) == 0

    img = images.reshape(2, rows, channels)
    cot = cotangent.reshape(2, rows, channels)
    choices = [(cells, cells - i) for i in range(cells)]
    choices += [(cells - i, cells) for i in range(1, cells)]

    def run(number, counts, img, cot, gains, depthwise, pointwise):
        used = choices[number]
        slots = sum(used)
        piece = half // 16
        landing = [
            pltpu.VMEM((slots, half // 2, channels), BF16),
            pltpu.VMEM((slots, half // 4, channels), BF16),
            pltpu.VMEM((slots, 3, piece, channels), BF16),
        ] + [pltpu.VMEM((slots, piece, channels), BF16)] * (bits - 4)
        steps = 9 + bits
        plan = (cells, used, False, bits, height, image_rows, per_core)
        grid_rows = (cells + 1, 8, channels)
        point, depth, gain = pl.pallas_call(
            functools.partial(kernel, plan),
            out_shape=(
                jax.ShapeDtypeStruct((cells, channels, channels), BF16),
                jax.ShapeDtypeStruct((9, cells, channels), F32),
                jax.ShapeDtypeStruct((cells, channels), F32),
            ),
            in_specs=[pl.BlockSpec(memory_space=pl.ANY)] * 2
            + [pl.BlockSpec(memory_space=pltpu.SMEM), pl.BlockSpec(memory_space=pltpu.VMEM)]
            + [pl.BlockSpec(memory_space=pl.ANY)] * 2,
            out_specs=(pl.BlockSpec(memory_space=pltpu.VMEM),) * 3,
            scratch_shapes=[
                pltpu.VMEM((2, 9, cells, channels), F32),
                pltpu.VMEM((2, 2 * cells, channels), F32),
                pltpu.VMEM((slots, channels, channels), BF16),
                pltpu.VMEM((slots + 1, rows, channels), BF16),
                pltpu.VMEM((slots, rows, LANES), F32),
                pltpu.VMEM((slots, rows, channels), F32),
                pltpu.VMEM((slots, rows, channels), F32),
                pltpu.VMEM((slots, rows, channels), BF16),
                pltpu.VMEM((rows, channels), BF16),
                pltpu.VMEM((rows, channels), F32),
                pltpu.VMEM((11, 8, channels), F32),
                pltpu.VMEM((9, 8, channels), F32),
                pltpu.VMEM((8, channels), F32),
                pltpu.VMEM((slots, channels, channels), BF16),
                pltpu.VMEM((slots, channels, channels), BF16),
                pltpu.VMEM((slots, half, channels), BF16),
                pltpu.VMEM((2,) + grid_rows, F32),
                pltpu.VMEM((bits + 1,) + grid_rows, F32),
                pltpu.VMEM((max(bits, 1),) + grid_rows, F32),
                pltpu.SemaphoreType.DMA((slots, steps)),
                pltpu.SemaphoreType.DMA((slots, steps)),
                pltpu.SemaphoreType.DMA((bits + 1,)),
                pltpu.SemaphoreType.DMA((bits + 1,)),
                pltpu.SemaphoreType.DMA((cells,)),
                pltpu.SemaphoreType.DMA((slots,)),
                pltpu.SemaphoreType.DMA((7,)),
            ]
            + landing,
            compiler_params=pltpu.CompilerParams(
                collective_id=number, has_side_effects=True, vmem_limit_bytes=60 * 1024 * 1024
            ),
        )(img, cot, counts, gains, depthwise.transpose(1, 0, 2), pointwise)
        return (point.astype(F32), depth.transpose(1, 0, 2), gain)

    other = lax.ppermute(counts, "section", [(0, 1), (1, 0)])
    is_first = lax.axis_index("section") == 0
    first = jnp.where(is_first, counts[0], other[0])
    second = jnp.where(is_first, other[0], counts[0])
    choice = jnp.where(first == cells, cells - second, 2 * cells - 1 - first)
    return lax.switch(
        choice,
        [functools.partial(run, number) for number in range(len(choices))],
        counts,
        img,
        cot,
        gains,
        depthwise,
        pointwise,
    )


def solution(mesh):
    placed = (
        P(None, "dp", None, None, None),
        P(None, "dp", None, None, None),
        P("section"),
        P("section", None),
        P("section", None, None),
        P("section", None, None),
    )
    return jax.shard_map(
        local,
        mesh=mesh,
        in_specs=placed,
        out_specs=(P("section", None, None), P("section", None, None), P("section", None)),
        check_vma=False,
    )
```

```python
import functools

import jax
import jax.numpy as jnp
from jax import lax
from jax.experimental import pallas as pl
from jax.experimental.pallas import tpu as pltpu
from jax.sharding import PartitionSpec as P

MESH = pl.DeviceIdType.MESH
EPSILON = 1e-06
LANES = 128
TILE = 16
F32 = jnp.float32
BF16 = jnp.bfloat16
PIECES = 4


def kernel(
    plan,
    img,
    cot,
    counts,
    gains,
    depth_in,
    point_in,
    out,
    depth_out,
    gain_out,
    depth,
    meta,
    point,
    xs,
    inv_all,
    normed_all,
    slope_all,
    act_all,
    gy,
    gl,
    taps,
    tap_acc,
    gain_acc,
    grads,
    reduced,
    from_core,
    small,
    small_recv,
    small_sum,
    send_sem,
    recv_sem,
    small_send,
    small_recv_sem,
    weight_send,
    weight_recv,
    load_sem,
    *landing,
):
    cells, used, masked, bits, height, image_rows, images = plan
    slots = sum(used)
    doublings = bits - 4
    rows = images * image_rows
    channels = point.shape[-1]
    half = channels // 2
    blocks = channels // LANES
    core = lax.axis_index("section")
    me = lax.axis_index("dp")
    sibling = 1 - core

    def owner(k):
        segment = (k + 8 - used[0]) // 8
        return segment, k - segment * used[0]

    digits = [lax.rem(me // (1 << b), 2) for b in range(bits)]
    weights = [1 << b for b in range(bits)]
    if bits >= 2:
        first, second = digits[0], digits[1]
        digits[0] = first + core * (second - first)
        digits[1] = second + core * (first - second)
        weights[0] = 1 + core
        weights[1] = 2 - core
    partners = [me + (1 - 2 * d) * w for d, w in zip(digits, weights)]
    base = core * half

    barrier = pltpu.get_barrier_semaphore()
    for home in (me, partners[1]):
        pl.semaphore_signal(barrier, inc=1, device_id=(sibling, home), device_id_type=MESH)
    ring = lax.rem(me // 4, 4)
    peers = [lax.rem(ring + r, 4) for r in range(4)]
    ring_partners = [me + (peer - ring) * 4 for peer in peers]
    for partner in partners[:2] + ring_partners[1:] + partners[4:]:
        pl.semaphore_signal(barrier, inc=1, device_id=(core, partner), device_id_type=MESH)

    load_img = pltpu.make_async_copy(img.at[core], xs.at[0], load_sem.at[0])
    load_cot = pltpu.make_async_copy(cot.at[core], gy, load_sem.at[1])
    load_depth = pltpu.make_async_copy(
        depth_in, depth.at[core], load_sem.at[2]
    )
    load_img.start()
    load_depth.start()

    def place(j):
        return core * used[0] + j

    def point_load(j):
        return pltpu.make_async_copy(
            point_in.at[j], point.at[place(j)], weight_recv.at[place(j)]
        )

    mine = used[0] + core * (used[1] - used[0])

    def each_cell(act):
        for j in range(cells):
            if j < min(used):
                act(j)
            elif j < max(used):

                @pl.when(core == (0 if used[0] > used[1] else 1))
                def _(j=j):
                    act(j)

    each_cell(lambda j: point_load(j).start())
    load_cot.start()
    for j in range(cells):
        meta[core, j : j + 1, :] = gains[j : j + 1, :]
        meta[core, cells + j : cells + j + 1, :] = jnp.where(
            jnp.full((1, channels), j, jnp.int32) < counts[0], 1.0, 0.0
        )
    pl.semaphore_wait(barrier, 3 + bits)

    def to_sibling(src, dst, send, recv):
        return pltpu.make_async_remote_copy(
            src_ref=src,
            dst_ref=dst,
            send_sem=send,
            recv_sem=recv,
            device_id=(sibling, me),
            device_id_type=MESH,
        )

    def depth_copy():
        return to_sibling(
            depth_in, depth.at[core], load_sem.at[3], load_sem.at[4]
        )

    def meta_copy():
        return to_sibling(meta.at[core], meta.at[core], load_sem.at[5], load_sem.at[6])

    def point_copy(j, part=slice(None)):
        return to_sibling(
            point_in.at[j, part],
            point.at[place(j), part],
            weight_send.at[j],
            weight_recv.at[place(j)],
        )

    def point_send(j):
        for piece in range(PIECES):
            point_copy(j, pl.ds(piece * (channels // PIECES), channels // PIECES)).start()

    depth_copy().start()
    meta_copy().start()
    point_send(0)
    load_img.wait()
    load_depth.wait()
    depth_copy().wait()
    meta_copy().wait()

    column = lax.broadcasted_iota(jnp.int32, (8, channels), 0)

    def set_taps(k, low_tap_edge, high_tap_edge):
        segment, j = owner(k)
        for p in range(3):
            for q in range(3):
                t = p * 3 + q
                tile = jnp.broadcast_to(
                    depth[segment, t, pl.ds(j, 1), :], (8, channels)
                )
                if q == 0:
                    tile = jnp.where(column == low_tap_edge, 0.0, tile)
                if q == 2:
                    tile = jnp.where(column == high_tap_edge, 0.0, tile)
                taps[t] = tile
        taps[9] = jnp.broadcast_to(meta[segment, pl.ds(j, 1), :], (8, channels))
        taps[10] = jnp.broadcast_to(meta[segment, pl.ds(cells + j, 1), :], (8, channels))

    def lane(block):
        return slice(block * LANES, (block + 1) * LANES)

    def stacked(tile, count):
        return jnp.concatenate([tile] * (count // 8), axis=0)

    def forward(k, carry):
        pltpu.make_async_copy(point.at[k], point.at[k], weight_recv.at[k]).wait()
        set_taps(k, 0, 7)

        def image(i, carry):
            at = pl.ds(pl.multiple_of(i * image_rows, image_rows), image_rows)
            xl = [xs[k, at, lane(b)].astype(F32) for b in range(blocks)]
            squares = sum(x * x for x in xl)
            mean = jnp.sum(squares, axis=1, keepdims=True) * (1.0 / channels)
            inv = jnp.broadcast_to(lax.rsqrt(mean + EPSILON), (image_rows, LANES))
            inv_all[k, at, :] = inv
            for b in range(blocks):
                normed = xl[b] * inv * stacked(taps[9, :, lane(b)], image_rows)
                normed_all[k, at, lane(b)] = normed
                mid = [normed[8 * h : 8 * h + 8] for h in range(height)]
                moved = [
                    [pltpu.roll(m, 1, axis=0) for m in mid],
                    mid,
                    [pltpu.roll(m, 7, axis=0) for m in mid],
                ]
                w = [taps[t, :, lane(b)] for t in range(9)]
                linear = []
                for h in range(height):
                    total = None
                    for p in range(3):
                        if 0 <= h + p - 1 < height:
                            for q in range(3):
                                term = w[p * 3 + q] * moved[q][h + p - 1]
                                total = term if total is None else total + term
                    linear.append(total)
                linear = jnp.concatenate(linear, axis=0)
                sigma = 0.5 * jnp.tanh(0.5 * linear) + 0.5
                act = linear * sigma
                act_all[k, at, lane(b)] = act.astype(BF16)
                slope_all[k, at, lane(b)] = sigma + act * (1.0 - sigma)
            return carry

        lax.fori_loop(0, images, image, 0, unroll=2)
        mixed = jnp.dot(act_all[k], point[k], preferred_element_type=F32)
        x = xs[k].astype(F32)
        y = x + mixed
        if masked:
            y = jnp.where(stacked(taps[10], rows) > 0.5, y, x)
        xs[k + 1] = y.astype(BF16)

        for j in range(1, cells):

            @pl.when((k == j - 1) & (j < mine))
            def _(j=j):
                point_copy(j - 1).wait_send()
                point_send(j)

        return carry

    lax.fori_loop(0, slots, forward, 0)
    load_cot.wait()
    for j in range(cells):

        @pl.when(j + 1 == mine)
        def _(j=j):
            point_copy(j).wait_send()


    def remote(src, dst, k, step, device):
        return pltpu.make_async_remote_copy(
            src_ref=src,
            dst_ref=dst,
            send_sem=send_sem.at[k, step],
            recv_sem=recv_sem.at[k, step],
            device_id=device,
            device_id_type=MESH,
        )

    def span(start, size):
        return pl.ds(pl.multiple_of(start, TILE), size)

    keep, away, sizes = [], [], []
    offset, size = base, half
    for b in range(2):
        size = size // 2
        away.append(offset + (1 - digits[b]) * size)
        offset = offset + digits[b] * size
        keep.append(offset)
        sizes.append(size)
    size = size // 4
    own = offset + ring * size

    def pieces(make, start, size, count):
        for piece in range(count):
            make(start + piece * (size // count), size // count).start()

    def core_copy(k, start, size):
        return remote(
            grads.at[k, span(sibling * half + start, size)],
            from_core.at[k, span(start, size)],
            k,
            0,
            (sibling, me),
        )

    def pair_copy(k, b, start, size):
        return remote(
            grads.at[k, span(away[b] + start, size)],
            landing[b].at[k, span(start, size)],
            k,
            1 + b,
            (core, partners[b]),
        )

    def send_pair(k, b):
        pieces(lambda start, size: pair_copy(k, b, start, size), 0, sizes[b], 2)

    def ring_copy(k, r):
        return remote(
            grads.at[k, span(offset + peers[r] * size, size)],
            landing[2].at[k, r - 1],
            k,
            2 + r,
            (core, ring_partners[r]),
        )

    def double_copy(k, d):
        return remote(
            grads.at[k, span(own, size)], landing[3 + d].at[k], k, 9 + d, (core, partners[4 + d])
        )

    def spread_copy(k, r):
        part = span(own, size)
        return remote(
            reduced.at[k, part],
            reduced.at[k, part],
            k,
            5 + r,
            (core, ring_partners[r]),
        )

    def gather_copy(k, b, start, size):
        part = span(keep[b] + start, size)
        return remote(
            reduced.at[k, part], reduced.at[k, part], k, 9 + doublings + b, (core, partners[b])
        )

    def send_gather(k, b):
        pieces(lambda start, size: gather_copy(k, b, start, size), 0, sizes[b], 2)

    homes = (me, partners[0])

    def home_copy(k, to, start, size):
        part = span(keep[0] + start, size)
        return remote(
            reduced.at[k, part],
            out.at[owner(k)[1], part],
            k,
            11 + doublings + to,
            (sibling, homes[to]),
        )

    def add_landed(k, part, *landed):
        total = grads[k, part].astype(F32)
        for block in landed:
            total = total + block.astype(F32)
        grads[k, part] = total.astype(BF16)

    def spread(k):
        part = span(own, size)
        reduced[k, part] = grads[k, part]
        for r in range(1, 4):
            spread_copy(k, r).start()

    def owned(k):
        return core == owner(k)[0]

    def send_home(k):
        @pl.when(owned(k))
        def _():
            send_gather(k, 0)

        @pl.when(core != owner(k)[0])
        def _():
            for to in (1, 0):
                pieces(
                    lambda start, size: home_copy(k, to, start, size), 0, sizes[0], PIECES // 2
                )

    def finish(k):
        @pl.when(owned(k))
        def _():
            part = span(base, half)
            gather_copy(k, 0, 0, sizes[0]).wait()
            out[owner(k)[1], part] = reduced[k, part]

    last_age = 7 + doublings

    def stage(k, age):
        if age == 1:
            core_copy(k, 0, half).wait()
            add_landed(k, span(base, half), from_core[k])
            send_pair(k, 0)
        elif age <= 3:
            b = age - 2
            pair_copy(k, b, 0, sizes[b]).wait()
            add_landed(k, span(keep[b], sizes[b]), landing[b][k])
            if b == 0:
                send_pair(k, 1)
            else:
                for r in range(1, 4):
                    ring_copy(k, r).start()
        elif age <= 4 + doublings:
            d = age - 4
            if d == 0:
                for r in range(1, 4):
                    ring_copy(k, r).wait()
                add_landed(k, span(own, size), *[landing[2][k, r] for r in range(3)])
            else:
                double_copy(k, d - 1).wait()
                add_landed(k, span(own, size), landing[2 + d][k])
            if d < doublings:
                double_copy(k, d).start()
            else:
                spread(k)
        elif age == 5 + doublings:
            for r in range(1, 4):
                spread_copy(k, r).wait()
            send_gather(k, 1)
        elif age == 6 + doublings:
            gather_copy(k, 1, 0, sizes[1]).wait()
            send_home(k)
        else:
            finish(k)

    def pump(n):
        order = list(range(4, 6 + doublings)) + [3, 6 + doublings, 2, 7 + doublings, 1]
        for age in order:

            @pl.when((n >= age) & (n < age + slots))
            def _(age=age):
                stage(slots - 1 - (n - age), age)

    def small_copy(step):
        if step == 0:
            src, device = small.at[sibling], (sibling, me)
        else:
            src, device = small_sum.at[step - 1], (core, partners[step - 1])
        return pltpu.make_async_remote_copy(
            src_ref=src,
            dst_ref=small_recv.at[step],
            send_sem=small_send.at[step],
            recv_sem=small_recv_sem.at[step],
            device_id=device,
            device_id_type=MESH,
        )

    def small_stage(age):
        small_copy(age - 1).wait()
        own = small[core] if age == 1 else small_sum[age - 2]
        total = own + small_recv[age - 1]
        if age <= bits:
            small_sum[age - 1] = total
            small_copy(age).start()
        else:
            for j in range(cells):
                for t in range(8):
                    depth_out[t, j : j + 1, :] = total[j, t : t + 1, :]
            depth_out[8] = total[cells, :cells]
            gain_out[...] = total[cells, cells:]

    small[...] = jnp.zeros_like(small)
    for j in range(cells):
        if j >= min(used):

            @pl.when(core == (0 if used[0] < used[1] else 1))
            def _(j=j):
                out[j] = jnp.zeros((channels, channels), BF16)

    def backward(n):
        k = slots - 1 - n
        gp = lax.dot_general(
            act_all[k], gy[...], (((0,), (0,)), ((), ())), preferred_element_type=F32
        )
        set_taps(k, 7, 0)
        if masked:
            gp = jnp.where(stacked(taps[10], channels) > 0.5, gp, 0.0)
        grads[k] = gp.astype(BF16)
        pieces(lambda start, size: core_copy(k, start, size), 0, half, PIECES)
        ga = lax.dot_general(
            gy[...], point[k], (((1,), (1,)), ((), ())), preferred_element_type=F32
        )
        gl[...] = ga * slope_all[k]
        tap_acc[...] = jnp.zeros_like(tap_acc)
        gain_acc[...] = jnp.zeros_like(gain_acc)

        def image(i, carry):
            at = pl.ds(pl.multiple_of(i * image_rows, image_rows), image_rows)
            inv = inv_all[k, at, :]
            gns = []
            for b in range(blocks):
                mid = [
                    gl[pl.ds(pl.multiple_of(i * image_rows + 8 * h, 8), 8), lane(b)]
                    for h in range(height)
                ]
                tiles = [
                    normed_all[
                        k, pl.ds(pl.multiple_of(i * image_rows + 8 * h, 8), 8), lane(b)
                    ]
                    for h in range(height)
                ]
                moved = [
                    [pltpu.roll(m, 7, axis=0) for m in mid],
                    mid,
                    [pltpu.roll(m, 1, axis=0) for m in mid],
                ]
                gn = [None] * height
                for p in range(3):
                    for q in range(3):
                        t = p * 3 + q
                        w = taps[t, :, lane(b)]
                        acc = tap_acc[t, :, lane(b)]
                        for h in range(height):
                            if 0 <= h - p + 1 < height:
                                piece = moved[q][h - p + 1]
                                term = w * piece
                                gn[h] = term if gn[h] is None else gn[h] + term
                                acc = acc + tiles[h] * piece
                        tap_acc[t, :, lane(b)] = acc
                gns.append(jnp.concatenate(gn, axis=0))
            dots = None
            us, xl = [], []
            for b in range(blocks):
                x = xs[k, at, lane(b)].astype(F32)
                term = gns[b] * x * inv
                gain_acc[:, lane(b)] += sum(term[8 * h : 8 * h + 8] for h in range(height))
                u = gns[b] * stacked(taps[9, :, lane(b)], image_rows)
                us.append(u)
                xl.append(x)
                dots = u * x if dots is None else dots + u * x
            mean = jnp.sum(dots, axis=1, keepdims=True) * (1.0 / channels)
            fall = jnp.broadcast_to(mean, (image_rows, LANES)) * (inv * inv * inv)
            for b in range(blocks):
                g = gy[at, lane(b)].astype(F32)
                gx = g + inv * us[b] - xl[b] * fall
                if masked:
                    gx = jnp.where(stacked(taps[10, :, lane(b)], image_rows) > 0.5, gx, g)
                gy[at, lane(b)] = gx.astype(BF16)
            return carry

        lax.fori_loop(0, images, image, 0, unroll=2)

        segment, j = owner(k)
        on = taps[10, 0:1, :] > 0.5
        sums = []
        for t in range(9):
            tile = tap_acc[t]
            if t % 3 == 0:
                tile = jnp.where(column == 7, 0.0, tile)
            if t % 3 == 2:
                tile = jnp.where(column == 0, 0.0, tile)
            total = jnp.sum(tile, axis=0, keepdims=True)
            sums.append(jnp.where(on, total, 0.0) if masked else total)
        gain = jnp.sum(gain_acc[...], axis=0, keepdims=True)
        if masked:
            gain = jnp.where(on, gain, 0.0)
        for t in range(8):
            small[segment, j, t : t + 1, :] = sums[t]
        small[segment, cells, pl.ds(j, 1), :] = sums[8]
        small[segment, cells, pl.ds(cells + j, 1), :] = gain

    def turn(n, carry):
        pump(n)

        @pl.when(n < slots)
        def _():
            backward(n)

        @pl.when(n == slots - 1)
        def _():
            small_copy(0).start()

        for age in range(1, bits + 2):

            @pl.when(n == slots - 1 + age)
            def _(age=age):
                small_stage(age)

        return carry

    lax.fori_loop(0, slots + max(last_age, bits + 1), turn, 0)

    def wait_home(n, carry):
        k = slots - 1 - n
        for to in (0, 1):

            @pl.when(core != owner(k)[0])
            def _(to=to):
                home_copy(k, to, 0, sizes[0]).wait_send()

            @pl.when(owned(k))
            def _(to=to):
                home_copy(k, to, 0, sizes[0]).wait_recv()

        return carry

    lax.fori_loop(0, slots, wait_home, 0)


def local(images, cotangent, counts, gains, depthwise, pointwise):
    cells, channels = gains.shape
    sections = lax.axis_size("section")
    replicas = lax.axis_size("dp")
    bits = replicas.bit_length() - 1
    assert sections == 2 and replicas == 1 << bits and cells == 4
    micro, batch, height, width = images.shape[:4]
    assert width == 8 and depthwise.shape[1] == 9
    image_rows = height * width
    per_core = micro * batch // 2
    rows = per_core * image_rows
    half = channels // 2
    assert bits >= 4 and half % (16 * TILE) == 0

    img = images.reshape(2, rows, channels)
    cot = cotangent.reshape(2, rows, channels)
    choices = [(cells, cells - i) for i in range(cells)]
    choices += [(cells - i, cells) for i in range(1, cells)]

    def run(number, counts, img, cot, gains, depthwise, pointwise):
        used = choices[number]
        slots = sum(used)
        piece = half // 16
        landing = [
            pltpu.VMEM((slots, half // 2, channels), BF16),
            pltpu.VMEM((slots, half // 4, channels), BF16),
            pltpu.VMEM((slots, 3, piece, channels), BF16),
        ] + [pltpu.VMEM((slots, piece, channels), BF16)] * (bits - 4)
        steps = 9 + bits
        plan = (cells, used, False, bits, height, image_rows, per_core)
        grid_rows = (cells + 1, 8, channels)
        point, depth, gain = pl.pallas_call(
            functools.partial(kernel, plan),
            out_shape=(
                jax.ShapeDtypeStruct((cells, channels, channels), BF16),
                jax.ShapeDtypeStruct((9, cells, channels), F32),
                jax.ShapeDtypeStruct((cells, channels), F32),
            ),
            in_specs=[pl.BlockSpec(memory_space=pl.ANY)] * 2
            + [pl.BlockSpec(memory_space=pltpu.SMEM), pl.BlockSpec(memory_space=pltpu.VMEM)]
            + [pl.BlockSpec(memory_space=pl.ANY)] * 2,
            out_specs=(pl.BlockSpec(memory_space=pltpu.VMEM),) * 3,
            scratch_shapes=[
                pltpu.VMEM((2, 9, cells, channels), F32),
                pltpu.VMEM((2, 2 * cells, channels), F32),
                pltpu.VMEM((slots, channels, channels), BF16),
                pltpu.VMEM((slots + 1, rows, channels), BF16),
                pltpu.VMEM((slots, rows, LANES), F32),
                pltpu.VMEM((slots, rows, channels), F32),
                pltpu.VMEM((slots, rows, channels), F32),
                pltpu.VMEM((slots, rows, channels), BF16),
                pltpu.VMEM((rows, channels), BF16),
                pltpu.VMEM((rows, channels), F32),
                pltpu.VMEM((11, 8, channels), F32),
                pltpu.VMEM((9, 8, channels), F32),
                pltpu.VMEM((8, channels), F32),
                pltpu.VMEM((slots, channels, channels), BF16),
                pltpu.VMEM((slots, channels, channels), BF16),
                pltpu.VMEM((slots, half, channels), BF16),
                pltpu.VMEM((2,) + grid_rows, F32),
                pltpu.VMEM((bits + 1,) + grid_rows, F32),
                pltpu.VMEM((max(bits, 1),) + grid_rows, F32),
                pltpu.SemaphoreType.DMA((slots, steps)),
                pltpu.SemaphoreType.DMA((slots, steps)),
                pltpu.SemaphoreType.DMA((bits + 1,)),
                pltpu.SemaphoreType.DMA((bits + 1,)),
                pltpu.SemaphoreType.DMA((cells,)),
                pltpu.SemaphoreType.DMA((slots,)),
                pltpu.SemaphoreType.DMA((7,)),
            ]
            + landing,
            compiler_params=pltpu.CompilerParams(
                collective_id=number, has_side_effects=True, vmem_limit_bytes=60 * 1024 * 1024
            ),
        )(img, cot, counts, gains, depthwise.transpose(1, 0, 2), pointwise)
        return (point.astype(F32), depth.transpose(1, 0, 2), gain)

    other = lax.ppermute(counts, "section", [(0, 1), (1, 0)])
    is_first = lax.axis_index("section") == 0
    first = jnp.where(is_first, counts[0], other[0])
    second = jnp.where(is_first, other[0], counts[0])
    choice = jnp.where(first == cells, cells - second, 2 * cells - 1 - first)
    return lax.switch(
        choice,
        [functools.partial(run, number) for number in range(len(choices))],
        counts,
        img,
        cot,
        gains,
        depthwise,
        pointwise,
    )


def solution(mesh):
    placed = (
        P(None, "dp", None, None, None),
        P(None, "dp", None, None, None),
        P("section"),
        P("section", None),
        P("section", None, None),
        P("section", None, None),
    )
    return jax.shard_map(
        local,
        mesh=mesh,
        in_specs=placed,
        out_specs=(P("section", None, None), P("section", None, None), P("section", None)),
        check_vma=False,
    )
```

```python
import functools

import jax
import jax.numpy as jnp
from jax import lax
from jax.experimental import pallas as pl
from jax.experimental.pallas import tpu as pltpu
from jax.sharding import PartitionSpec as P

MESH = pl.DeviceIdType.MESH
EPSILON = 1e-06
LANES = 128
TILE = 16
F32 = jnp.float32
BF16 = jnp.bfloat16
PIECES = 8


def kernel(
    plan,
    img,
    cot,
    counts,
    gains,
    depth_in,
    point_in,
    out,
    depth_out,
    gain_out,
    depth,
    meta,
    point,
    xs,
    inv_all,
    normed_all,
    slope_all,
    act_all,
    gy,
    gl,
    taps,
    tap_acc,
    gain_acc,
    grads,
    reduced,
    from_core,
    small,
    small_recv,
    small_sum,
    send_sem,
    recv_sem,
    small_send,
    small_recv_sem,
    weight_send,
    weight_recv,
    load_sem,
    *landing,
):
    cells, used, masked, bits, height, image_rows, images = plan
    slots = sum(used)
    doublings = bits - 4
    rows = images * image_rows
    channels = point.shape[-1]
    half = channels // 2
    blocks = channels // LANES
    core = lax.axis_index("section")
    me = lax.axis_index("dp")
    sibling = 1 - core

    def owner(k):
        segment = (k + 8 - used[0]) // 8
        return segment, k - segment * used[0]

    digits = [lax.rem(me // (1 << b), 2) for b in range(bits)]
    weights = [1 << b for b in range(bits)]
    if bits >= 2:
        first, second = digits[0], digits[1]
        digits[0] = first + core * (second - first)
        digits[1] = second + core * (first - second)
        weights[0] = 1 + core
        weights[1] = 2 - core
    partners = [me + (1 - 2 * d) * w for d, w in zip(digits, weights)]
    base = core * half

    barrier = pltpu.get_barrier_semaphore()
    for home in (me, partners[1]):
        pl.semaphore_signal(barrier, inc=1, device_id=(sibling, home), device_id_type=MESH)
    ring = lax.rem(me // 4, 4)
    peers = [lax.rem(ring + r, 4) for r in range(4)]
    ring_partners = [me + (peer - ring) * 4 for peer in peers]
    for partner in partners[:2] + ring_partners[1:] + partners[4:]:
        pl.semaphore_signal(barrier, inc=1, device_id=(core, partner), device_id_type=MESH)

    load_img = pltpu.make_async_copy(img.at[core], xs.at[0], load_sem.at[0])
    load_cot = pltpu.make_async_copy(cot.at[core], gy, load_sem.at[1])
    load_depth = pltpu.make_async_copy(
        depth_in, depth.at[core], load_sem.at[2]
    )
    load_img.start()
    load_depth.start()

    def place(j):
        return core * used[0] + j

    def point_load(j):
        return pltpu.make_async_copy(
            point_in.at[j], point.at[place(j)], weight_recv.at[place(j)]
        )

    def each_cell(act):
        for j in range(cells):
            if j < min(used):
                act(j)
            elif j < max(used):

                @pl.when(core == (0 if used[0] > used[1] else 1))
                def _(j=j):
                    act(j)

    each_cell(lambda j: point_load(j).start())
    load_cot.start()
    for j in range(cells):
        meta[core, j : j + 1, :] = gains[j : j + 1, :]
        meta[core, cells + j : cells + j + 1, :] = jnp.where(
            jnp.full((1, channels), j, jnp.int32) < counts[0], 1.0, 0.0
        )
    pl.semaphore_wait(barrier, 3 + bits)

    def to_sibling(src, dst, send, recv):
        return pltpu.make_async_remote_copy(
            src_ref=src,
            dst_ref=dst,
            send_sem=send,
            recv_sem=recv,
            device_id=(sibling, me),
            device_id_type=MESH,
        )

    def depth_copy():
        return to_sibling(
            depth_in, depth.at[core], load_sem.at[3], load_sem.at[4]
        )

    def meta_copy():
        return to_sibling(meta.at[core], meta.at[core], load_sem.at[5], load_sem.at[6])

    def point_copy(j, part=slice(None)):
        return to_sibling(
            point_in.at[j, part],
            point.at[place(j), part],
            weight_send.at[j],
            weight_recv.at[place(j)],
        )

    def point_send(j):
        for piece in range(PIECES):
            point_copy(j, pl.ds(piece * (channels // PIECES), channels // PIECES)).start()

    depth_copy().start()
    meta_copy().start()
    each_cell(point_send)
    load_img.wait()
    load_depth.wait()
    depth_copy().wait()
    meta_copy().wait()

    column = lax.broadcasted_iota(jnp.int32, (8, channels), 0)

    def set_taps(k, low_tap_edge, high_tap_edge):
        segment, j = owner(k)
        for p in range(3):
            for q in range(3):
                t = p * 3 + q
                tile = jnp.broadcast_to(
                    depth[segment, t, pl.ds(j, 1), :], (8, channels)
                )
                if q == 0:
                    tile = jnp.where(column == low_tap_edge, 0.0, tile)
                if q == 2:
                    tile = jnp.where(column == high_tap_edge, 0.0, tile)
                taps[t] = tile
        taps[9] = jnp.broadcast_to(meta[segment, pl.ds(j, 1), :], (8, channels))
        taps[10] = jnp.broadcast_to(meta[segment, pl.ds(cells + j, 1), :], (8, channels))

    def lane(block):
        return slice(block * LANES, (block + 1) * LANES)

    def stacked(tile, count):
        return jnp.concatenate([tile] * (count // 8), axis=0)

    def forward(k, carry):
        pltpu.make_async_copy(point.at[k], point.at[k], weight_recv.at[k]).wait()
        set_taps(k, 0, 7)

        def image(i, carry):
            at = pl.ds(pl.multiple_of(i * image_rows, image_rows), image_rows)
            xl = [xs[k, at, lane(b)].astype(F32) for b in range(blocks)]
            squares = sum(x * x for x in xl)
            mean = jnp.sum(squares, axis=1, keepdims=True) * (1.0 / channels)
            inv = jnp.broadcast_to(lax.rsqrt(mean + EPSILON), (image_rows, LANES))
            inv_all[k, at, :] = inv
            for b in range(blocks):
                normed = xl[b] * inv * stacked(taps[9, :, lane(b)], image_rows)
                normed_all[k, at, lane(b)] = normed
                mid = [normed[8 * h : 8 * h + 8] for h in range(height)]
                moved = [
                    [pltpu.roll(m, 1, axis=0) for m in mid],
                    mid,
                    [pltpu.roll(m, 7, axis=0) for m in mid],
                ]
                w = [taps[t, :, lane(b)] for t in range(9)]
                linear = []
                for h in range(height):
                    total = None
                    for p in range(3):
                        if 0 <= h + p - 1 < height:
                            for q in range(3):
                                term = w[p * 3 + q] * moved[q][h + p - 1]
                                total = term if total is None else total + term
                    linear.append(total)
                linear = jnp.concatenate(linear, axis=0)
                sigma = 0.5 * jnp.tanh(0.5 * linear) + 0.5
                act = linear * sigma
                act_all[k, at, lane(b)] = act.astype(BF16)
                slope_all[k, at, lane(b)] = sigma + act * (1.0 - sigma)
            return carry

        lax.fori_loop(0, images, image, 0, unroll=2)
        mixed = jnp.dot(act_all[k], point[k], preferred_element_type=F32)
        x = xs[k].astype(F32)
        y = x + mixed
        if masked:
            y = jnp.where(stacked(taps[10], rows) > 0.5, y, x)
        xs[k + 1] = y.astype(BF16)
        return carry

    lax.fori_loop(0, slots, forward, 0)
    load_cot.wait()
    each_cell(lambda j: point_copy(j).wait_send())

    def remote(src, dst, k, step, device):
        return pltpu.make_async_remote_copy(
            src_ref=src,
            dst_ref=dst,
            send_sem=send_sem.at[k, step],
            recv_sem=recv_sem.at[k, step],
            device_id=device,
            device_id_type=MESH,
        )

    def span(start, size):
        return pl.ds(pl.multiple_of(start, TILE), size)

    keep, away, sizes = [], [], []
    offset, size = base, half
    for b in range(2):
        size = size // 2
        away.append(offset + (1 - digits[b]) * size)
        offset = offset + digits[b] * size
        keep.append(offset)
        sizes.append(size)
    size = size // 4
    own = offset + ring * size

    def pieces(make, start, size, count):
        for piece in range(count):
            make(start + piece * (size // count), size // count).start()

    def core_copy(k, start, size):
        return remote(
            grads.at[k, span(sibling * half + start, size)],
            from_core.at[k, span(start, size)],
            k,
            0,
            (sibling, me),
        )

    def pair_copy(k, b, start, size):
        return remote(
            grads.at[k, span(away[b] + start, size)],
            landing[b].at[k, span(start, size)],
            k,
            1 + b,
            (core, partners[b]),
        )

    def send_pair(k, b):
        pieces(lambda start, size: pair_copy(k, b, start, size), 0, sizes[b], 4)

    def ring_copy(k, r):
        return remote(
            grads.at[k, span(offset + peers[r] * size, size)],
            landing[2].at[k, r - 1],
            k,
            2 + r,
            (core, ring_partners[r]),
        )

    def double_copy(k, d):
        return remote(
            grads.at[k, span(own, size)], landing[3 + d].at[k], k, 9 + d, (core, partners[4 + d])
        )

    def spread_copy(k, r):
        part = span(own, size)
        return remote(
            reduced.at[k, part],
            reduced.at[k, part],
            k,
            5 + r,
            (core, ring_partners[r]),
        )

    def gather_copy(k, b, start, size):
        part = span(keep[b] + start, size)
        return remote(
            reduced.at[k, part], reduced.at[k, part], k, 9 + doublings + b, (core, partners[b])
        )

    def send_gather(k, b):
        pieces(lambda start, size: gather_copy(k, b, start, size), 0, sizes[b], 4)

    homes = (me, partners[0])

    def home_copy(k, to, start, size):
        part = span(keep[0] + start, size)
        return remote(
            reduced.at[k, part],
            out.at[owner(k)[1], part],
            k,
            11 + doublings + to,
            (sibling, homes[to]),
        )

    def add_landed(k, part, *landed):
        total = grads[k, part].astype(F32)
        for block in landed:
            total = total + block.astype(F32)
        grads[k, part] = total.astype(BF16)

    def spread(k):
        part = span(own, size)
        reduced[k, part] = grads[k, part]
        for r in range(1, 4):
            spread_copy(k, r).start()

    def owned(k):
        return core == owner(k)[0]

    def send_home(k):
        @pl.when(owned(k))
        def _():
            send_gather(k, 0)

        @pl.when(core != owner(k)[0])
        def _():
            for to in (1, 0):
                pieces(
                    lambda start, size: home_copy(k, to, start, size), 0, sizes[0], PIECES // 2
                )

    def finish(k):
        @pl.when(owned(k))
        def _():
            part = span(base, half)
            gather_copy(k, 0, 0, sizes[0]).wait()
            out[owner(k)[1], part] = reduced[k, part]

    last_age = 7 + doublings

    def stage(k, age):
        if age == 1:
            core_copy(k, 0, half).wait()
            add_landed(k, span(base, half), from_core[k])
            send_pair(k, 0)
        elif age <= 3:
            b = age - 2
            pair_copy(k, b, 0, sizes[b]).wait()
            add_landed(k, span(keep[b], sizes[b]), landing[b][k])
            if b == 0:
                send_pair(k, 1)
            else:
                for r in range(1, 4):
                    ring_copy(k, r).start()
        elif age <= 4 + doublings:
            d = age - 4
            if d == 0:
                for r in range(1, 4):
                    ring_copy(k, r).wait()
                add_landed(k, span(own, size), *[landing[2][k, r] for r in range(3)])
            else:
                double_copy(k, d - 1).wait()
                add_landed(k, span(own, size), landing[2 + d][k])
            if d < doublings:
                double_copy(k, d).start()
            else:
                spread(k)
        elif age == 5 + doublings:
            for r in range(1, 4):
                spread_copy(k, r).wait()
            send_gather(k, 1)
        elif age == 6 + doublings:
            gather_copy(k, 1, 0, sizes[1]).wait()
            send_home(k)
        else:
            finish(k)

    def pump(n):
        order = list(range(4, 6 + doublings)) + [3, 6 + doublings, 2, 7 + doublings, 1]
        for age in order:

            @pl.when((n >= age) & (n < age + slots))
            def _(age=age):
                stage(slots - 1 - (n - age), age)

    def small_copy(step):
        if step == 0:
            src, device = small.at[sibling], (sibling, me)
        else:
            src, device = small_sum.at[step - 1], (core, partners[step - 1])
        return pltpu.make_async_remote_copy(
            src_ref=src,
            dst_ref=small_recv.at[step],
            send_sem=small_send.at[step],
            recv_sem=small_recv_sem.at[step],
            device_id=device,
            device_id_type=MESH,
        )

    def small_stage(age):
        small_copy(age - 1).wait()
        own = small[core] if age == 1 else small_sum[age - 2]
        total = own + small_recv[age - 1]
        if age <= bits:
            small_sum[age - 1] = total
            small_copy(age).start()
        else:
            for j in range(cells):
                for t in range(8):
                    depth_out[t, j : j + 1, :] = total[j, t : t + 1, :]
            depth_out[8] = total[cells, :cells]
            gain_out[...] = total[cells, cells:]

    small[...] = jnp.zeros_like(small)
    for j in range(cells):
        if j >= min(used):

            @pl.when(core == (0 if used[0] < used[1] else 1))
            def _(j=j):
                out[j] = jnp.zeros((channels, channels), BF16)

    def backward(n):
        k = slots - 1 - n
        gp = lax.dot_general(
            act_all[k], gy[...], (((0,), (0,)), ((), ())), preferred_element_type=F32
        )
        set_taps(k, 7, 0)
        if masked:
            gp = jnp.where(stacked(taps[10], channels) > 0.5, gp, 0.0)
        grads[k] = gp.astype(BF16)
        pieces(lambda start, size: core_copy(k, start, size), 0, half, PIECES)
        ga = lax.dot_general(
            gy[...], point[k], (((1,), (1,)), ((), ())), preferred_element_type=F32
        )
        gl[...] = ga * slope_all[k]
        tap_acc[...] = jnp.zeros_like(tap_acc)
        gain_acc[...] = jnp.zeros_like(gain_acc)

        def image(i, carry):
            at = pl.ds(pl.multiple_of(i * image_rows, image_rows), image_rows)
            inv = inv_all[k, at, :]
            gns = []
            for b in range(blocks):
                mid = [
                    gl[pl.ds(pl.multiple_of(i * image_rows + 8 * h, 8), 8), lane(b)]
                    for h in range(height)
                ]
                tiles = [
                    normed_all[
                        k, pl.ds(pl.multiple_of(i * image_rows + 8 * h, 8), 8), lane(b)
                    ]
                    for h in range(height)
                ]
                moved = [
                    [pltpu.roll(m, 7, axis=0) for m in mid],
                    mid,
                    [pltpu.roll(m, 1, axis=0) for m in mid],
                ]
                gn = [None] * height
                for p in range(3):
                    for q in range(3):
                        t = p * 3 + q
                        w = taps[t, :, lane(b)]
                        acc = tap_acc[t, :, lane(b)]
                        for h in range(height):
                            if 0 <= h - p + 1 < height:
                                piece = moved[q][h - p + 1]
                                term = w * piece
                                gn[h] = term if gn[h] is None else gn[h] + term
                                acc = acc + tiles[h] * piece
                        tap_acc[t, :, lane(b)] = acc
                gns.append(jnp.concatenate(gn, axis=0))
            dots = None
            us, xl = [], []
            for b in range(blocks):
                x = xs[k, at, lane(b)].astype(F32)
                term = gns[b] * x * inv
                gain_acc[:, lane(b)] += sum(term[8 * h : 8 * h + 8] for h in range(height))
                u = gns[b] * stacked(taps[9, :, lane(b)], image_rows)
                us.append(u)
                xl.append(x)
                dots = u * x if dots is None else dots + u * x
            mean = jnp.sum(dots, axis=1, keepdims=True) * (1.0 / channels)
            fall = jnp.broadcast_to(mean, (image_rows, LANES)) * (inv * inv * inv)
            for b in range(blocks):
                g = gy[at, lane(b)].astype(F32)
                gx = g + inv * us[b] - xl[b] * fall
                if masked:
                    gx = jnp.where(stacked(taps[10, :, lane(b)], image_rows) > 0.5, gx, g)
                gy[at, lane(b)] = gx.astype(BF16)
            return carry

        lax.fori_loop(0, images, image, 0, unroll=2)

        segment, j = owner(k)
        on = taps[10, 0:1, :] > 0.5
        sums = []
        for t in range(9):
            tile = tap_acc[t]
            if t % 3 == 0:
                tile = jnp.where(column == 7, 0.0, tile)
            if t % 3 == 2:
                tile = jnp.where(column == 0, 0.0, tile)
            total = jnp.sum(tile, axis=0, keepdims=True)
            sums.append(jnp.where(on, total, 0.0) if masked else total)
        gain = jnp.sum(gain_acc[...], axis=0, keepdims=True)
        if masked:
            gain = jnp.where(on, gain, 0.0)
        for t in range(8):
            small[segment, j, t : t + 1, :] = sums[t]
        small[segment, cells, pl.ds(j, 1), :] = sums[8]
        small[segment, cells, pl.ds(cells + j, 1), :] = gain

    def turn(n, carry):
        pump(n)

        @pl.when(n < slots)
        def _():
            backward(n)

        @pl.when(n == slots - 1)
        def _():
            small_copy(0).start()

        for age in range(1, bits + 2):

            @pl.when(n == slots - 1 + age)
            def _(age=age):
                small_stage(age)

        return carry

    lax.fori_loop(0, slots + max(last_age, bits + 1), turn, 0)

    def wait_home(n, carry):
        k = slots - 1 - n
        for to in (0, 1):

            @pl.when(core != owner(k)[0])
            def _(to=to):
                home_copy(k, to, 0, sizes[0]).wait_send()

            @pl.when(owned(k))
            def _(to=to):
                home_copy(k, to, 0, sizes[0]).wait_recv()

        return carry

    lax.fori_loop(0, slots, wait_home, 0)


def local(images, cotangent, counts, gains, depthwise, pointwise):
    cells, channels = gains.shape
    sections = lax.axis_size("section")
    replicas = lax.axis_size("dp")
    bits = replicas.bit_length() - 1
    assert sections == 2 and replicas == 1 << bits and cells == 4
    micro, batch, height, width = images.shape[:4]
    assert width == 8 and depthwise.shape[1] == 9
    image_rows = height * width
    per_core = micro * batch // 2
    rows = per_core * image_rows
    half = channels // 2
    assert bits >= 4 and half % (16 * TILE) == 0

    img = images.reshape(2, rows, channels)
    cot = cotangent.reshape(2, rows, channels)
    choices = [(cells, cells - i) for i in range(cells)]
    choices += [(cells - i, cells) for i in range(1, cells)]

    def run(number, counts, img, cot, gains, depthwise, pointwise):
        used = choices[number]
        slots = sum(used)
        piece = half // 16
        landing = [
            pltpu.VMEM((slots, half // 2, channels), BF16),
            pltpu.VMEM((slots, half // 4, channels), BF16),
            pltpu.VMEM((slots, 3, piece, channels), BF16),
        ] + [pltpu.VMEM((slots, piece, channels), BF16)] * (bits - 4)
        steps = 9 + bits
        plan = (cells, used, False, bits, height, image_rows, per_core)
        grid_rows = (cells + 1, 8, channels)
        point, depth, gain = pl.pallas_call(
            functools.partial(kernel, plan),
            out_shape=(
                jax.ShapeDtypeStruct((cells, channels, channels), BF16),
                jax.ShapeDtypeStruct((9, cells, channels), F32),
                jax.ShapeDtypeStruct((cells, channels), F32),
            ),
            in_specs=[pl.BlockSpec(memory_space=pl.ANY)] * 2
            + [pl.BlockSpec(memory_space=pltpu.SMEM), pl.BlockSpec(memory_space=pltpu.VMEM)]
            + [pl.BlockSpec(memory_space=pl.ANY)] * 2,
            out_specs=(pl.BlockSpec(memory_space=pltpu.VMEM),) * 3,
            scratch_shapes=[
                pltpu.VMEM((2, 9, cells, channels), F32),
                pltpu.VMEM((2, 2 * cells, channels), F32),
                pltpu.VMEM((slots, channels, channels), BF16),
                pltpu.VMEM((slots + 1, rows, channels), BF16),
                pltpu.VMEM((slots, rows, LANES), F32),
                pltpu.VMEM((slots, rows, channels), F32),
                pltpu.VMEM((slots, rows, channels), F32),
                pltpu.VMEM((slots, rows, channels), BF16),
                pltpu.VMEM((rows, channels), BF16),
                pltpu.VMEM((rows, channels), F32),
                pltpu.VMEM((11, 8, channels), F32),
                pltpu.VMEM((9, 8, channels), F32),
                pltpu.VMEM((8, channels), F32),
                pltpu.VMEM((slots, channels, channels), BF16),
                pltpu.VMEM((slots, channels, channels), BF16),
                pltpu.VMEM((slots, half, channels), BF16),
                pltpu.VMEM((2,) + grid_rows, F32),
                pltpu.VMEM((bits + 1,) + grid_rows, F32),
                pltpu.VMEM((max(bits, 1),) + grid_rows, F32),
                pltpu.SemaphoreType.DMA((slots, steps)),
                pltpu.SemaphoreType.DMA((slots, steps)),
                pltpu.SemaphoreType.DMA((bits + 1,)),
                pltpu.SemaphoreType.DMA((bits + 1,)),
                pltpu.SemaphoreType.DMA((cells,)),
                pltpu.SemaphoreType.DMA((slots,)),
                pltpu.SemaphoreType.DMA((7,)),
            ]
            + landing,
            compiler_params=pltpu.CompilerParams(
                collective_id=number, has_side_effects=True, vmem_limit_bytes=60 * 1024 * 1024
            ),
        )(img, cot, counts, gains, depthwise.transpose(1, 0, 2), pointwise)
        return (point.astype(F32), depth.transpose(1, 0, 2), gain)

    other = lax.ppermute(counts, "section", [(0, 1), (1, 0)])
    is_first = lax.axis_index("section") == 0
    first = jnp.where(is_first, counts[0], other[0])
    second = jnp.where(is_first, other[0], counts[0])
    choice = jnp.where(first == cells, cells - second, 2 * cells - 1 - first)
    return lax.switch(
        choice,
        [functools.partial(run, number) for number in range(len(choices))],
        counts,
        img,
        cot,
        gains,
        depthwise,
        pointwise,
    )


def solution(mesh):
    placed = (
        P(None, "dp", None, None, None),
        P(None, "dp", None, None, None),
        P("section"),
        P("section", None),
        P("section", None, None),
        P("section", None, None),
    )
    return jax.shard_map(
        local,
        mesh=mesh,
        in_specs=placed,
        out_specs=(P("section", None, None), P("section", None, None), P("section", None)),
        check_vma=False,
    )
```
